32 devices in a mesh: slab: 16 (over z, y, x), col: 2 (over core).
Axes of the slice: x: 2, y: 2, z: 4, core: 2. Of those that a mesh axis runs over, the one named last changes fastest.
Arguments:
- displacement: float32 [3, 64, 128, 256], P(None, 'slab', 'col'), may hold values from -6 to 6
- velocity: float32 [3, 64, 128, 256], P(None, 'slab', 'col'), may hold values from -6 to 6
- damage: float32 [64, 128, 256], P('slab', 'col'), may hold values from 0.5 to 1.5
- broken: int32 [2, 64, 128, 256], P(None, 'slab', 'col'), may hold values from 0 to 255, as said below
- counts: int32 [16, 4], replicated, may hold values from 0 to 64, as said below
- bits: int32 [4], replicated, may hold values from 0 to 3, each once
Outputs:
- relocated: float32 [6, 64, 128, 256], P(None, 'slab', 'col')
The draws below stay inside these ranges and needn't reach their ends.
Inputs may be any that keep to these rules, and one draw needn't show every extreme that they name: Each bit of a plane of broken marks one forward bond as broken. `counts`: in every aligned group of 16 slabs, the slabs at offsets 0, 1, 2, 4 and 8 of the group offer 64 columns in every round. `bits`: each bit 0..3 is used in exactly one round.
All inputs are finite; a program needn't handle non-finite values.
Results may differ from the reference program's by a relative error of at most 0.00002.
Values sent between devices are 32-bit elements; how exact they have to be, the bound alone decides.
A program may use at most 64 MiB of HBM per device.

```python
import math
import jax
import jax.numpy as jnp

CX = 4
CYH = 64
ROUNDS = 4
SLABS = 16
MAXC = 64
NX = 64
NY = 128
NZ = 256
N_COL = 2


def draw_broken(key, part):
    total = jnp.zeros((2, NX, NY, NZ), jnp.int32)
    for index in range(8):
        picked = jax.random.randint(jax.random.fold_in(key, index), (2, NX, NY, NZ), 0, 20)
        total = total + jnp.left_shift(jnp.where(picked < 3, 1, 0).astype(jnp.int32), index)
    chosen = jax.random.randint(jax.random.fold_in(key, 99), (), 0, NX * NY * NZ)
    flat_index = jnp.arange(NX * NY * NZ, dtype=jnp.int32).reshape(1, NX, NY, NZ)
    return jnp.where(flat_index == chosen, 255, total).astype(jnp.int32)


def draw_counts(key, part):
    base = jax.random.randint(key, (SLABS, ROUNDS), 0, MAXC + 1)
    place = jnp.arange(SLABS) % 16
    filled = (place == 0) | (place == 1) | (place == 2) | (place == 4) | (place == 8)
    return jnp.where(filled[:, None], MAXC, base).astype(jnp.int32)


def shard_levels(own_key, extent, split, least, high):
    factor_of, own = 1.0, jax.random.fold_in(own_key, 6)
    for position, shards_of in split:
        heights = jnp.exp(jax.random.uniform(jax.random.fold_in(own, position), (shards_of,), jnp.float32, least / len(split), high / len(split)))
        factor_of = factor_of * jnp.repeat(heights, extent[position] // shards_of).reshape([-1 if axis == position else 1 for axis in range(len(extent))])
    return factor_of


def centred(own_key, shape, scale, most, split=(), kind=jnp.bfloat16):
    values = scale * jax.random.normal(own_key, shape, jnp.float32)
    if split:
        values = values * shard_levels(own_key, shape, split, -0.22, 0.18)
    return jnp.clip(values, -most, most).astype(kind)


def setup_inputs(seed: int = 0) -> dict:
    streams_of = jax.random.split(jax.random.key(seed), 7)
    displacement = centred(streams_of[0], (3, NX, NY, NZ), 1.0, 6.0, ((1, 16), (2, 2)), jnp.float32)
    velocity = centred(streams_of[1], (3, NX, NY, NZ), 1.0, 6.0, ((1, 16), (2, 2)), jnp.float32)
    damage = jnp.clip(0.5 + 1.0 * jax.random.uniform(streams_of[2], (NX, NY, NZ), jnp.float32) ** shard_levels(streams_of[2], (NX, NY, NZ), ((0, 16), (1, 2)), -0.2, 0.2), 0.5, 1.5)
    broken = draw_broken(jax.random.fold_in(streams_of[6], 71), 0)
    counts = draw_counts(jax.random.fold_in(streams_of[6], 71), 0)
    bits = jax.random.permutation(streams_of[5], ROUNDS).astype(jnp.int32)
    return {"displacement": displacement, "velocity": velocity, "damage": damage, "broken": broken, "counts": counts, "bits": bits}


def bond_table():
    table = []
    for step_x in range(-2, 3):
        for step_y in range(-2, 3):
            for step_z in range(-2, 3):
                square = step_x * step_x + step_y * step_y + step_z * step_z
                if 0 < square <= 4 and (step_x, step_y, step_z) > (0, 0, 0):
                    length = math.sqrt(square)
                    table.append((step_x, step_y, step_z, (1.0 - length / 2.5) / length ** 3))
    return table

def reference(displacement, velocity, damage, broken, counts, bits):
    extent_x, extent_y, extent_z = damage.shape
    moved = jnp.pad(displacement, ((0, 0), (2, 2), (2, 2), (2, 2)))
    scaled = jnp.pad(damage, 2)
    flags = jnp.pad(broken, ((0, 0), (2, 2), (2, 2), (2, 2)))
    force = jnp.zeros(displacement.shape, jnp.float32)
    for index, (step_x, step_y, step_z, weight) in enumerate(bond_table()):
        plane_index = index // 8
        bit_index = index % 8
        for sign in (1, -1):
            low_x, low_y, low_z = (2 + sign * step_x, 2 + sign * step_y, 2 + sign * step_z)
            other = moved[:, low_x:low_x + extent_x, low_y:low_y + extent_y, low_z:low_z + extent_z]
            other_scale = scaled[low_x:low_x + extent_x, low_y:low_y + extent_y, low_z:low_z + extent_z]
            if sign == 1:
                source = broken[plane_index]
            else:
                source = flags[plane_index, low_x:low_x + extent_x, low_y:low_y + extent_y, low_z:low_z + extent_z]
            alive = 1.0 - jnp.bitwise_and(jnp.right_shift(source, bit_index), 1).astype(jnp.float32)
            along = step_x * (other[0] - displacement[0]) + step_y * (other[1] - displacement[1]) + step_z * (other[2] - displacement[2])
            factor = weight * damage * other_scale * alive * along
            force = force + jnp.stack([factor * step_x, factor * step_y, factor * step_z])
    new_velocity = velocity + 0.1 * force
    new_displacement = displacement + 0.1 * new_velocity
    state = jnp.concatenate([new_displacement, new_velocity], 0)
    blocks = state.reshape(6, SLABS, CX, N_COL, CYH, extent_z).transpose(1, 3, 0, 2, 4, 5)
    blocks = blocks.reshape(SLABS, N_COL, 6, CX * CYH, extent_z)
    device = jnp.arange(SLABS, dtype=jnp.int32)
    column = jnp.arange(CX * CYH, dtype=jnp.int32)
    for round_index in range(ROUNDS):
        shift = jnp.left_shift(jnp.int32(1), bits[round_index].astype(jnp.int32)).astype(jnp.int32)
        partner = jnp.bitwise_xor(device, shift).astype(jnp.int32)
        taken = jnp.minimum(counts[:, round_index], jnp.take(counts[:, round_index], partner))
        other = jnp.take(blocks, partner, axis=0)
        keep = column[None, :] < taken[:, None]
        blocks = jnp.where(keep[:, None, None, :, None], other, blocks)
    blocks = blocks.reshape(SLABS, N_COL, 6, CX, CYH, extent_z).transpose(2, 0, 3, 1, 4, 5)
    return blocks.reshape(6, extent_x, extent_y, extent_z)
```

```python
import functools
import math

import jax
import jax.numpy as jnp
from jax import lax
from jax.experimental import pallas as pl
from jax.experimental.pallas import tpu as pltpu
from jax.sharding import PartitionSpec as P

MESH = pl.DeviceIdType.MESH
PLACE = (0, 2, 3)
BAND = 16
ROUNDS = 4


def bond_table():
    table = []
    for step_x in range(-2, 3):
        for step_y in range(-2, 3):
            for step_z in range(-2, 3):
                square = step_x * step_x + step_y * step_y + step_z * step_z
                if 0 < square <= 4 and (step_x, step_y, step_z) > (0, 0, 0):
                    length = math.sqrt(square)
                    table.append((step_x, step_y, step_z, (1.0 - length / 2.5) / length**3))
    return table


def moved_along_cells(value, step):
    cells = value.shape[-1]
    lane = lax.broadcasted_iota(jnp.int32, value.shape, value.ndim - 1)
    turned = pltpu.roll(value, (-step) % cells, value.ndim - 1)
    inside = (lane < cells - step) if step > 0 else (lane >= -step)
    return jnp.where(inside, turned, jnp.zeros_like(turned))


def kernel(
    taken, bits, rounds_of, displacement, velocity, damage, broken, result,
    fields, flags, fields_low, fields_high, flags_low, flags_high,
    rows_low, rows_high, row_flags_low, row_flags_high, far_low, far_high, far_flags,
    partial, back, returned, stage, arrived, ready_velocity,
    in00, in01, in10, in11, out00, out01, out10, out11,
    col_send, col_recv, down_send, down_recv, back_send, back_recv,
    ride_send, ride_recv,
):
    planes, rows, cells = damage.shape
    half = cells // 2
    slabs = lax.axis_size("slab")
    slab = lax.axis_index("slab")
    col = lax.axis_index("col")
    other = 1 - col
    has_low = slab > 0
    has_high = slab < slabs - 1
    table = bond_table()
    incoming = ((in00, in01), (in10, in11))
    outgoing = ((out00, out01), (out10, out11))

    for component in range(3):
        fields[PLACE[component], 0:planes, 8 : 8 + rows] = displacement[component]
    fields[1, 0:planes, 8 : 8 + rows] = damage[...]
    flags[:, :, 8 : 8 + rows] = broken[...]
    fields[:, 0:planes, 0:8] = jnp.zeros((4, planes, 8, cells), jnp.float32)
    fields[:, 0:planes, 8 + rows : 16 + rows] = jnp.zeros((4, planes, 8, cells), jnp.float32)
    fields[:, planes : planes + 2] = jnp.zeros((4, 2, rows + 16, cells), jnp.float32)
    flags[:, :, 0:8] = jnp.zeros((2, planes, 8, cells), jnp.int32)
    flags[:, :, 8 + rows : 16 + rows] = jnp.zeros((2, planes, 8, cells), jnp.int32)
    returned[...] = jnp.zeros_like(returned)
    stage[...] = jnp.zeros_like(stage)

    partners = []
    for bit in range(ROUNDS):
        weight = 1 << bit
        partners.append(slab + weight - 2 * weight * ((slab // weight) % 2))

    barrier = pltpu.get_barrier_semaphore()

    def greet(to_slab, to_col):
        pl.semaphore_signal(barrier, inc=1, device_id=(to_slab, to_col), device_id_type=MESH)

    greet(slab, other)
    for partner in partners:
        greet(partner, col)

    @pl.when(has_low)
    def _():
        greet(slab - 1, col)
        greet(slab - 1, other)

    @pl.when(has_high)
    def _():
        greet(slab + 1, col)
        greet(slab + 1, other)

    sides = has_low.astype(jnp.int32) + has_high.astype(jnp.int32)
    pl.semaphore_wait(barrier, 1 + ROUNDS + 2 * sides)

    rim = pl.ds(pl.multiple_of(8 + (1 - col) * (rows - 8), 8), 8)
    ghost = pl.ds(pl.multiple_of((8 + rows) * col, 8), 8)

    def remote(source, target, sends, receives, to_slab, to_col):
        return pltpu.make_async_remote_copy(
            src_ref=source, dst_ref=target, send_sem=sends, recv_sem=receives,
            device_id=(to_slab, to_col), device_id_type=MESH,
        )

    beside = [
        remote(fields.at[:, 0:planes, rim], fields.at[:, 0:planes, ghost],
               col_send.at[0], col_recv.at[0], slab, other),
        remote(flags.at[:, :, rim], flags.at[:, :, ghost],
               col_send.at[1], col_recv.at[1], slab, other),
    ]
    inner = pl.ds(8, rows)
    below = [
        remote(fields.at[:, 0, inner], fields.at[:, planes, inner],
               down_send.at[0], down_recv.at[0], slab - 1, col),
        remote(fields.at[:, 0, rim], fields.at[:, planes, ghost],
               down_send.at[1], down_recv.at[1], slab - 1, other),
        remote(fields.at[0:2, 1, inner], fields.at[0:2, planes + 1, inner],
               down_send.at[2], down_recv.at[2], slab - 1, col),
    ]
    above = [
        remote(back.at[0:3], returned.at[0:3], back_send.at[0], back_recv.at[0], slab + 1, col),
        remote(back.at[3], returned.at[3], back_send.at[1], back_recv.at[1], slab + 1, col),
    ]

    @pl.when(has_low)
    def _():
        for copy in below:
            copy.start()

    for copy in beside:
        copy.start()

    column = lax.broadcasted_iota(jnp.int32, (rows, half), 0)

    def rides(pipe, step):
        parity = step % 2
        return [
            remote(outgoing[pipe][parity].at[bit], incoming[pipe][parity].at[bit],
                   ride_send.at[pipe, parity, bit], ride_recv.at[pipe, parity, bit],
                   partners[bit], col)
            for bit in range(ROUNDS)
        ]

    last = 6 + ROUNDS - 1

    def ride(pipe, step):
        lanes = slice(pipe * half, (pipe + 1) * half)
        if step > 0:
            for copy in rides(pipe, step - 1):
                copy.wait_recv()
            source = incoming[pipe][(step - 1) % 2]
            for number in reversed(range(ROUNDS)):
                new = jnp.where(
                    column < taken[number], source[bits[number]], stage[pipe, number]
                )
                if number < ROUNDS - 1:
                    stage[pipe, number + 1] = new
                elif step >= ROUNDS:
                    item = step - ROUNDS
                    if item < 3:
                        arrived[item, :, lanes] = new
                    else:
                        result[item, 0, :, lanes] = new
                        result[item - 3, 0, :, lanes] = arrived[item - 3, :, lanes] + 0.1 * new
        if step < last:
            if step < 3:
                stage[pipe, 0] = displacement[step, 0, :, lanes]
            elif step < 6:
                stage[pipe, 0] = ready_velocity[step - 3, :, lanes]
            if step >= 2:
                for copy in rides(pipe, step - 2):
                    copy.wait_send()
            target = outgoing[pipe][step % 2]
            for bit in range(ROUNDS):
                target[bit] = stage[pipe, rounds_of[bit]]
            for copy in rides(pipe, step):
                copy.start()
        else:
            for back_step in (last - 2, last - 1):
                for copy in rides(pipe, back_step):
                    copy.wait_send()

    def ride_both(step):
        for pipe in range(2):
            ride(pipe, step)

    def shift_plane(plane, with_flags):
        def body(index, carry):
            here = pl.ds(pl.multiple_of(index * 8, 8), 8)
            for field in range(4):
                value = fields[field, plane, here]
                fields_low[field, plane, here] = moved_along_cells(value, -1)
                fields_high[field, plane, here] = moved_along_cells(value, 1)
            if with_flags:
                for part in range(2):
                    value = flags[part, plane, here]
                    flags_low[part, plane, here] = moved_along_cells(value, -1)
                    flags_high[part, plane, here] = moved_along_cells(value, 1)
            return carry

        lax.fori_loop(0, (rows + 16) // 8, body, 0)

        def field_rows(field, carry):
            for place, source in enumerate((fields_low, fields, fields_high)):
                rows_low[place, field, plane] = source[field, plane, 7 : 7 + rows]
                rows_high[place, field, plane] = source[field, plane, 9 : 9 + rows]
            return carry

        lax.fori_loop(0, 4, field_rows, 0)
        if with_flags:

            def flag_rows(part, carry):
                for place, source in enumerate((flags_low, flags, flags_high)):
                    row_flags_low[place, part, plane] = source[part, plane, 7 : 7 + rows]
                    row_flags_high[place, part, plane] = source[part, plane, 9 : 9 + rows]
                return carry

            lax.fori_loop(0, 2, flag_rows, 0)
            for field in range(2):
                far_low[field, plane] = fields[field + 1, plane, 6 : 6 + rows]
                far_high[field, plane] = fields[field + 1, plane, 10 : 10 + rows]
            far_flags[plane] = flags[0, plane, 6 : 6 + rows]

    def force_on(plane, choose, emit):
        def body(index, carry):
            start = pl.multiple_of(index * BAND, 8)
            own_rows = pl.ds(start + 8, BAND)
            own = [fields[field, plane, own_rows] for field in range(4)]
            force = [jnp.zeros((BAND, cells), jnp.float32) for _ in range(3)]
            for number, (step_x, step_y, step_z, weight) in enumerate(table):
                for sign in (1, -1):
                    if not choose(step_x, sign):
                        continue
                    step = (sign * step_x, sign * step_y, sign * step_z)
                    there = plane + step[0]

                    def load(plain, low, high, less, more, far_less, far_more, first):
                        if step[1] == -2:
                            return far_less(first, there)
                        if step[1] == 2:
                            return far_more(first, there)
                        if step[1] != 0:
                            shifted = less if step[1] < 0 else more
                            return shifted[step[2] + 1, first, there, pl.ds(start, BAND)]
                        if step[2] == 0:
                            return plain[first, there, own_rows]
                        if step[2] == 1:
                            return high[first, there, own_rows]
                        if step[2] == -1:
                            return low[first, there, own_rows]
                        return moved_along_cells(plain[first, there, own_rows], step[2])

                    def field_at(first):
                        return load(
                            fields, fields_low, fields_high, rows_low, rows_high,
                            lambda f, p: far_low[f - 1, p, pl.ds(start, BAND)],
                            lambda f, p: far_high[f - 1, p, pl.ds(start, BAND)],
                            first,
                        )

                    along = None
                    for component in range(3):
                        if step[component] == 0:
                            continue
                        part = field_at(PLACE[component])
                        part = part - own[PLACE[component]]
                        if step[component] < 0:
                            part = -part
                        along = part if along is None else along + part
                    size = 2.0 if max(abs(s) for s in step) == 2 else 1.0
                    scale = field_at(1)
                    if sign == 1:
                        source = flags[number // 8, plane, own_rows]
                    else:
                        source = load(
                            flags, flags_low, flags_high, row_flags_low, row_flags_high,
                            lambda f, p: far_flags[p, pl.ds(start, BAND)], None, number // 8,
                        )
                    factor = (weight * size * size) * scale * along
                    factor = jnp.where(
                        jnp.bitwise_and(source, 1 << (number % 8)) == 0, factor, 0.0
                    )
                    for component in range(3):
                        if step[component] > 0:
                            force[component] = force[component] + factor
                        elif step[component] < 0:
                            force[component] = force[component] - factor
            emit(pl.ds(start, BAND), [own[1] * total for total in force])
            return carry

        lax.fori_loop(0, rows // BAND, body, 0)

    def keep_partial(plane):
        def emit(where, force):
            for component in range(3):
                partial[plane, component, where] = force[component]
        return emit

    def finish(plane):
        def emit(where, force):
            for component in range(3):
                new = velocity[component, plane, where] + 0.1 * force[component]
                result[3 + component, plane, where] = new
                result[component, plane, where] = (
                    displacement[component, plane, where] + 0.1 * new
                )
        return emit

    ride_both(0)
    for copy in beside:
        copy.wait()
    for plane in range(planes):
        shift_plane(plane, True)
    ride_both(1)
    force_on(0, lambda step_x, sign: sign == 1 or step_x == 0, keep_partial(0))
    force_on(1, lambda step_x, sign: sign == 1 or step_x <= 1, keep_partial(1))
    ride_both(2)

    @pl.when(has_low)
    def _():
        for copy in below:
            copy.wait_send()

    @pl.when(has_high)
    def _():
        for copy in below:
            copy.wait_recv()

    shift_plane(planes, False)

    def keep_back(where, force):
        for component in range(3):
            back[component, where] = force[component]

    def keep_far(where, force):
        back[3, where] = force[0]

    force_on(planes, lambda step_x, sign: sign == -1 and step_x > 0, keep_back)

    @pl.when(has_high)
    def _():
        above[0].start()

    force_on(planes + 1, lambda step_x, sign: sign == -1 and step_x == 2, keep_far)

    @pl.when(has_high)
    def _():
        above[1].start()

    for plane in range(2, planes):
        force_on(plane, lambda step_x, sign: True, finish(plane))

    @pl.when(has_low)
    def _():
        above[0].wait_recv()

    for component in range(3):
        total = partial[0, component] + returned[component]
        ready_velocity[component] = velocity[component, 0] + 0.1 * total
    ride_both(3)

    @pl.when(has_low)
    def _():
        above[1].wait_recv()

    @pl.when(has_high)
    def _():
        for copy in above:
            copy.wait_send()

    for component in range(3):
        total = partial[1, component]
        if component == 0:
            total = total + returned[3]
        new = velocity[component, 1] + 0.1 * total
        result[3 + component, 1] = new
        result[component, 1] = displacement[component, 1] + 0.1 * new
    for step in range(4, last + 1):
        ride_both(step)


def on_device(displacement, velocity, damage, broken, counts, bits):
    planes, rows, cells = damage.shape
    half = cells // 2
    slab = lax.axis_index("slab")
    steps = jnp.arange(ROUNDS)
    partner = jnp.bitwise_xor(slab, jnp.left_shift(jnp.int32(1), bits))
    taken = jnp.minimum(counts[slab], counts[partner, steps])
    rounds_of = jnp.sum(
        jnp.where(bits[None, :] == steps[:, None], steps[None, :], 0), axis=1
    ).astype(jnp.int32)
    vmem = pl.BlockSpec(memory_space=pltpu.VMEM)
    smem = pl.BlockSpec(memory_space=pltpu.SMEM)
    f32, i32 = jnp.float32, jnp.int32
    tall = rows + 16
    return pl.pallas_call(
        kernel,
        out_shape=jax.ShapeDtypeStruct((6, planes, rows, cells), f32),
        in_specs=[smem] * 3 + [vmem] * 4,
        out_specs=vmem,
        scratch_shapes=[
            pltpu.VMEM((4, planes + 2, tall, cells), f32),
            pltpu.VMEM((2, planes, tall, cells), i32),
            pltpu.VMEM((4, planes + 1, tall, cells), f32),
            pltpu.VMEM((4, planes + 1, tall, cells), f32),
            pltpu.VMEM((2, planes, tall, cells), i32),
            pltpu.VMEM((2, planes, tall, cells), i32),
            pltpu.VMEM((3, 4, planes + 1, rows, cells), f32),
            pltpu.VMEM((3, 4, planes + 1, rows, cells), f32),
            pltpu.VMEM((3, 2, planes, rows, cells), i32),
            pltpu.VMEM((3, 2, planes, rows, cells), i32),
            pltpu.VMEM((2, planes, rows, cells), f32),
            pltpu.VMEM((2, planes, rows, cells), f32),
            pltpu.VMEM((planes, rows, cells), i32),
            pltpu.VMEM((2, 3, rows, cells), f32),
            pltpu.VMEM((4, rows, cells), f32),
            pltpu.VMEM((4, rows, cells), f32),
            pltpu.VMEM((2, ROUNDS, rows, half), f32),
            pltpu.VMEM((3, rows, cells), f32),
            pltpu.VMEM((3, rows, cells), f32),
        ]
        + [pltpu.VMEM((ROUNDS, rows, half), f32)] * 8
        + [
            pltpu.SemaphoreType.DMA((2,)),
            pltpu.SemaphoreType.DMA((2,)),
            pltpu.SemaphoreType.DMA((3,)),
            pltpu.SemaphoreType.DMA((3,)),
            pltpu.SemaphoreType.DMA((2,)),
            pltpu.SemaphoreType.DMA((2,)),
            pltpu.SemaphoreType.DMA((2, 2, ROUNDS)),
            pltpu.SemaphoreType.DMA((2, 2, ROUNDS)),
        ],
        compiler_params=pltpu.CompilerParams(
            collective_id=0, has_side_effects=True, vmem_limit_bytes=48 * 1024 * 1024
        ),
    )(taken, bits, rounds_of, displacement, velocity, damage, broken)


def solution(mesh):
    return jax.shard_map(
        on_device,
        mesh=mesh,
        in_specs=(
            P(None, "slab", "col", None),
            P(None, "slab", "col", None),
            P("slab", "col", None),
            P(None, "slab", "col", None),
            P(),
            P(),
        ),
        out_specs=P(None, "slab", "col", None),
        check_vma=False,
    )
```

```python
import functools
import math

import jax
import jax.numpy as jnp
from jax import lax
from jax.experimental import pallas as pl
from jax.experimental.pallas import tpu as pltpu
from jax.sharding import PartitionSpec as P

MESH = pl.DeviceIdType.MESH
PLACE = (0, 2, 3)
BAND = 16
ROUNDS = 4
PIPES = 4
PARTS = 4


def bond_table():
    table = []
    for step_x in range(-2, 3):
        for step_y in range(-2, 3):
            for step_z in range(-2, 3):
                square = step_x * step_x + step_y * step_y + step_z * step_z
                if 0 < square <= 4 and (step_x, step_y, step_z) > (0, 0, 0):
                    length = math.sqrt(square)
                    table.append((step_x, step_y, step_z, (1.0 - length / 2.5) / length**3))
    return table


def moved_along_cells(value, step):
    cells = value.shape[-1]
    lane = lax.broadcasted_iota(jnp.int32, value.shape, value.ndim - 1)
    turned = pltpu.roll(value, (-step) % cells, value.ndim - 1)
    inside = (lane < cells - step) if step > 0 else (lane >= -step)
    return jnp.where(inside, turned, jnp.zeros_like(turned))


def kernel(
    counts, bits, displacement, velocity_in, damage, broken, result,
    fields, flags, velocity, fields_low, fields_high, flags_low, flags_high,
    rows_low, rows_high, row_flags_low, row_flags_high, far_low, far_high, far_flags,
    partial, back, returned, stage, arrived, ready_velocity, *rest,
):
    buffers, rest = rest[: 4 * PIPES], rest[4 * PIPES :]
    (
        col_send, col_recv, down_send, down_recv, back_send, back_recv,
        ride_send, ride_recv, load_done,
    ) = rest
    planes, rows, cells = damage.shape
    half = cells // 2
    slabs = lax.axis_size("slab")
    slab = lax.axis_index("slab")
    col = lax.axis_index("col")
    other = 1 - col
    has_low = slab > 0
    has_high = slab < slabs - 1
    table = bond_table()
    incoming = [buffers[2 * pipe : 2 * pipe + 2] for pipe in range(PIPES)]
    outgoing = [buffers[2 * (PIPES + pipe) : 2 * (PIPES + pipe) + 2] for pipe in range(PIPES)]

    inner = pl.ds(8, rows)
    loads = [
        pltpu.make_async_copy(
            displacement.at[component], fields.at[PLACE[component], 0:planes, inner],
            load_done.at[component],
        )
        for component in range(3)
    ]
    loads.append(
        pltpu.make_async_copy(damage, fields.at[1, 0:planes, inner], load_done.at[3])
    )
    load_flags = pltpu.make_async_copy(broken, flags.at[:, :, inner], load_done.at[4])
    load_velocity = pltpu.make_async_copy(velocity_in, velocity, load_done.at[5])
    for copy in loads + [load_flags, load_velocity]:
        copy.start()
    fields[:, 0:planes, 0:8] = jnp.zeros((4, planes, 8, cells), jnp.float32)
    fields[:, 0:planes, 8 + rows : 16 + rows] = jnp.zeros((4, planes, 8, cells), jnp.float32)
    fields[:, planes : planes + 2] = jnp.zeros((4, 2, rows + 16, cells), jnp.float32)
    flags[:, :, 0:8] = jnp.zeros((2, planes, 8, cells), jnp.int32)
    flags[:, :, 8 + rows : 16 + rows] = jnp.zeros((2, planes, 8, cells), jnp.int32)
    returned[...] = jnp.zeros_like(returned)
    stage[...] = jnp.zeros_like(stage)

    partners = []
    for bit in range(ROUNDS):
        weight = 1 << bit
        partners.append(slab + weight - 2 * weight * ((slab // weight) % 2))

    taken, rounds_of = [], []
    for number in range(ROUNDS):
        partner = partners[0]
        for bit in range(1, ROUNDS):
            partner = jnp.where(bits[number] == bit, partners[bit], partner)
        taken.append(jnp.minimum(counts[slab, number], counts[partner, number]))
    for bit in range(ROUNDS):
        place = jnp.int32(0)
        for number in range(1, ROUNDS):
            place = jnp.where(bits[number] == bit, number, place)
        rounds_of.append(place)

    barrier = pltpu.get_barrier_semaphore()

    def greet(to_slab, to_col):
        pl.semaphore_signal(barrier, inc=1, device_id=(to_slab, to_col), device_id_type=MESH)

    greet(slab, other)
    for partner in partners:
        greet(partner, col)

    @pl.when(has_low)
    def _():
        greet(slab - 1, col)
        greet(slab - 1, other)

    @pl.when(has_high)
    def _():
        greet(slab + 1, col)
        greet(slab + 1, other)

    sides = has_low.astype(jnp.int32) + has_high.astype(jnp.int32)
    pl.semaphore_wait(barrier, 1 + ROUNDS + 2 * sides)

    rim = pl.ds(pl.multiple_of(8 + (1 - col) * (rows - 8), 8), 8)
    ghost = pl.ds(pl.multiple_of((8 + rows) * col, 8), 8)

    def remote(source, target, sends, receives, to_slab, to_col):
        return pltpu.make_async_remote_copy(
            src_ref=source, dst_ref=target, send_sem=sends, recv_sem=receives,
            device_id=(to_slab, to_col), device_id_type=MESH,
        )

    beside = [
        remote(fields.at[:, 0:planes, rim], fields.at[:, 0:planes, ghost],
               col_send.at[0], col_recv.at[0], slab, other),
        remote(flags.at[:, :, rim], flags.at[:, :, ghost],
               col_send.at[1], col_recv.at[1], slab, other),
    ]
    below = [
        remote(fields.at[:, 0, inner], fields.at[:, planes, inner],
               down_send.at[0], down_recv.at[0], slab - 1, col),
        remote(fields.at[:, 0, rim], fields.at[:, planes, ghost],
               down_send.at[1], down_recv.at[1], slab - 1, other),
        remote(fields.at[0:2, 1, inner], fields.at[0:2, planes + 1, inner],
               down_send.at[2], down_recv.at[2], slab - 1, col),
    ]
    above = [
        remote(back.at[0:3], returned.at[0:3], back_send.at[0], back_recv.at[0], slab + 1, col),
        remote(back.at[3], returned.at[3], back_send.at[1], back_recv.at[1], slab + 1, col),
    ]

    for copy in loads:
        copy.wait()

    @pl.when(has_low)
    def _():
        for copy in below:
            copy.start()

    beside[0].start()
    load_flags.wait()
    beside[1].start()

    column = lax.broadcasted_iota(jnp.int32, (3, 8, half), 1)

    def rides(pipe, step):
        parity = step % 2
        return [
            remote(outgoing[pipe][parity].at[bit], incoming[pipe][parity].at[bit],
                   ride_send.at[pipe, parity, bit], ride_recv.at[pipe, parity, bit],
                   partners[bit], col)
            for bit in range(ROUNDS)
        ]

    last = 2 * PARTS + ROUNDS - 1

    def ride(pipe, step):
        def spot(item):
            part = item % PARTS
            first = pipe * (rows // PIPES) + (part // 2) * 8
            return slice(first, first + 8), slice(part % 2 * half, (part % 2 + 1) * half)

        if step > 0:
            for copy in rides(pipe, step - 1):
                copy.wait_recv()
            source = incoming[pipe][(step - 1) % 2]
            for number in reversed(range(ROUNDS)):
                item = step - 1 - number
                if not 0 <= item < 2 * PARTS:
                    continue
                where, lanes = spot(item)
                new = jnp.where(
                    column < taken[number] - where.start,
                    source[bits[number]], stage[pipe, number],
                )
                if number < ROUNDS - 1:
                    stage[pipe, number + 1] = new
                elif item < PARTS:
                    arrived[:, where, lanes] = new
                else:
                    result[3:6, 0, where, lanes] = new
                    result[0:3, 0, where, lanes] = arrived[:, where, lanes] + 0.1 * new
        if step < last:
            if step < 2 * PARTS:
                where, lanes = spot(step)
                if step < PARTS:
                    tall = slice(where.start + 8, where.stop + 8)
                    for component in range(3):
                        stage[pipe, 0, component] = fields[PLACE[component], 0, tall, lanes]
                else:
                    stage[pipe, 0] = ready_velocity[:, where, lanes]
            if step >= 2:
                for copy in rides(pipe, step - 2):
                    copy.wait_send()
            target = outgoing[pipe][step % 2]
            for bit in range(ROUNDS):
                target[bit] = stage[pipe, rounds_of[bit]]
            for copy in rides(pipe, step):
                copy.start()
        else:
            for back_step in (last - 2, last - 1):
                for copy in rides(pipe, back_step):
                    copy.wait_send()

    def ride_both(step):
        for pipe in range(PIPES):
            ride(pipe, step)

    def shift_plane(plane, with_flags):
        for field in range(4):
            value = fields[field, plane]
            fields_low[field, plane] = moved_along_cells(value, -1)
            fields_high[field, plane] = moved_along_cells(value, 1)
        if with_flags:
            for part in range(2):
                value = flags[part, plane]
                flags_low[part, plane] = moved_along_cells(value, -1)
                flags_high[part, plane] = moved_along_cells(value, 1)

        def field_rows(field, carry):
            for place, source in enumerate((fields_low, fields, fields_high)):
                rows_low[place, field, plane] = source[field, plane, 7 : 7 + rows]
                rows_high[place, field, plane] = source[field, plane, 9 : 9 + rows]
            return carry

        lax.fori_loop(0, 4, field_rows, 0)
        if with_flags:

            def flag_rows(part, carry):
                for place, source in enumerate((flags_low, flags, flags_high)):
                    row_flags_low[place, part, plane] = source[part, plane, 7 : 7 + rows]
                    row_flags_high[place, part, plane] = source[part, plane, 9 : 9 + rows]
                return carry

            lax.fori_loop(0, 2, flag_rows, 0)
            for field in range(2):
                far_low[field, plane] = fields[field + 1, plane, 6 : 6 + rows]
                far_high[field, plane] = fields[field + 1, plane, 10 : 10 + rows]
            far_flags[plane] = flags[0, plane, 6 : 6 + rows]

    def force_on(plane, choose, emit):
        def body(index, carry):
            start = pl.multiple_of(index * BAND, 8)
            own_rows = pl.ds(start + 8, BAND)
            own = [fields[field, plane, own_rows] for field in range(4)]
            force = [jnp.zeros((BAND, cells), jnp.float32) for _ in range(3)]
            for number, (step_x, step_y, step_z, weight) in enumerate(table):
                for sign in (1, -1):
                    if not choose(step_x, sign):
                        continue
                    step = (sign * step_x, sign * step_y, sign * step_z)
                    there = plane + step[0]

                    def load(plain, low, high, less, more, far_less, far_more, first):
                        if step[1] == -2:
                            return far_less(first, there)
                        if step[1] == 2:
                            return far_more(first, there)
                        if step[1] != 0:
                            shifted = less if step[1] < 0 else more
                            return shifted[step[2] + 1, first, there, pl.ds(start, BAND)]
                        if step[2] == 0:
                            return plain[first, there, own_rows]
                        if step[2] == 1:
                            return high[first, there, own_rows]
                        if step[2] == -1:
                            return low[first, there, own_rows]
                        return moved_along_cells(plain[first, there, own_rows], step[2])

                    def field_at(first):
                        return load(
                            fields, fields_low, fields_high, rows_low, rows_high,
                            lambda f, p: far_low[f - 1, p, pl.ds(start, BAND)],
                            lambda f, p: far_high[f - 1, p, pl.ds(start, BAND)],
                            first,
                        )

                    along = None
                    for component in range(3):
                        if step[component] == 0:
                            continue
                        part = field_at(PLACE[component])
                        part = part - own[PLACE[component]]
                        if step[component] < 0:
                            part = -part
                        along = part if along is None else along + part
                    size = 2.0 if max(abs(s) for s in step) == 2 else 1.0
                    scale = field_at(1)
                    if sign == 1:
                        source = flags[number // 8, plane, own_rows]
                    else:
                        source = load(
                            flags, flags_low, flags_high, row_flags_low, row_flags_high,
                            lambda f, p: far_flags[p, pl.ds(start, BAND)], None, number // 8,
                        )
                    factor = (weight * size * size) * scale * along
                    factor = jnp.where(
                        jnp.bitwise_and(source, 1 << (number % 8)) == 0, factor, 0.0
                    )
                    for component in range(3):
                        if step[component] > 0:
                            force[component] = force[component] + factor
                        elif step[component] < 0:
                            force[component] = force[component] - factor
            emit(pl.ds(start, BAND), [own[1] * total for total in force])
            return carry

        lax.fori_loop(0, rows // BAND, body, 0)

    def keep_partial(plane):
        def emit(where, force):
            for component in range(3):
                partial[plane, component, where] = force[component]
        return emit

    def finish(plane):
        def emit(where, force):
            for component in range(3):
                new = velocity[component, plane, where] + 0.1 * force[component]
                result[3 + component, plane, where] = new
                result[component, plane, where] = (
                    fields[PLACE[component], plane, pl.ds(where.start + 8, BAND)] + 0.1 * new
                )
        return emit

    ride_both(0)
    for copy in beside:
        copy.wait()
    ride_both(1)

    def shift_own(plane, carry):
        shift_plane(plane, True)
        return carry

    lax.fori_loop(0, planes, shift_own, 0)
    ride_both(2)
    force_on(0, lambda step_x, sign: sign == 1 or step_x == 0, keep_partial(0))
    force_on(1, lambda step_x, sign: sign == 1 or step_x <= 1, keep_partial(1))
    ride_both(3)

    @pl.when(has_low)
    def _():
        for copy in below:
            copy.wait_send()

    @pl.when(has_high)
    def _():
        for copy in below:
            copy.wait_recv()

    shift_plane(planes, False)

    def keep_back(where, force):
        for component in range(3):
            back[component, where] = force[component]

    def keep_far(where, force):
        back[3, where] = force[0]

    force_on(planes, lambda step_x, sign: sign == -1 and step_x > 0, keep_back)

    @pl.when(has_high)
    def _():
        above[0].start()

    force_on(planes + 1, lambda step_x, sign: sign == -1 and step_x == 2, keep_far)

    @pl.when(has_high)
    def _():
        above[1].start()

    load_velocity.wait()
    for plane in range(2, planes):
        force_on(plane, lambda step_x, sign: True, finish(plane))

    @pl.when(has_low)
    def _():
        above[0].wait_recv()

    for component in range(3):
        total = partial[0, component] + returned[component]
        ready_velocity[component] = velocity[component, 0] + 0.1 * total
    ride_both(PARTS)

    @pl.when(has_low)
    def _():
        above[1].wait_recv()

    @pl.when(has_high)
    def _():
        for copy in above:
            copy.wait_send()

    for component in range(3):
        total = partial[1, component]
        if component == 0:
            total = total + returned[3]
        new = velocity[component, 1] + 0.1 * total
        result[3 + component, 1] = new
        result[component, 1] = fields[PLACE[component], 1, 8 : 8 + rows] + 0.1 * new
    for step in range(PARTS + 1, last + 1):
        ride_both(step)


def on_device(displacement, velocity, damage, broken, counts, bits):
    planes, rows, cells = damage.shape
    half = cells // 2
    vmem = pl.BlockSpec(memory_space=pltpu.VMEM)
    smem = pl.BlockSpec(memory_space=pltpu.SMEM)
    hbm = pl.BlockSpec(memory_space=pltpu.HBM)
    f32, i32 = jnp.float32, jnp.int32
    tall = rows + 16
    return pl.pallas_call(
        kernel,
        out_shape=jax.ShapeDtypeStruct((6, planes, rows, cells), f32),
        in_specs=[smem] * 2 + [hbm] * 4,
        out_specs=vmem,
        scratch_shapes=[
            pltpu.VMEM((4, planes + 2, tall, cells), f32),
            pltpu.VMEM((2, planes, tall, cells), i32),
            pltpu.VMEM((3, planes, rows, cells), f32),
            pltpu.VMEM((4, planes + 1, tall, cells), f32),
            pltpu.VMEM((4, planes + 1, tall, cells), f32),
            pltpu.VMEM((2, planes, tall, cells), i32),
            pltpu.VMEM((2, planes, tall, cells), i32),
            pltpu.VMEM((3, 4, planes + 1, rows, cells), f32),
            pltpu.VMEM((3, 4, planes + 1, rows, cells), f32),
            pltpu.VMEM((3, 2, planes, rows, cells), i32),
            pltpu.VMEM((3, 2, planes, rows, cells), i32),
            pltpu.VMEM((2, planes, rows, cells), f32),
            pltpu.VMEM((2, planes, rows, cells), f32),
            pltpu.VMEM((planes, rows, cells), i32),
            pltpu.VMEM((2, 3, rows, cells), f32),
            pltpu.VMEM((4, rows, cells), f32),
            pltpu.VMEM((4, rows, cells), f32),
            pltpu.VMEM((PIPES, ROUNDS, 3, 8, half), f32),
            pltpu.VMEM((3, rows, cells), f32),
            pltpu.VMEM((3, rows, cells), f32),
        ]
        + [pltpu.VMEM((ROUNDS, 3, 8, half), f32)] * (4 * PIPES)
        + [
            pltpu.SemaphoreType.DMA((2,)),
            pltpu.SemaphoreType.DMA((2,)),
            pltpu.SemaphoreType.DMA((3,)),
            pltpu.SemaphoreType.DMA((3,)),
            pltpu.SemaphoreType.DMA((2,)),
            pltpu.SemaphoreType.DMA((2,)),
            pltpu.SemaphoreType.DMA((PIPES, 2, ROUNDS)),
            pltpu.SemaphoreType.DMA((PIPES, 2, ROUNDS)),
            pltpu.SemaphoreType.DMA((6,)),
        ],
        compiler_params=pltpu.CompilerParams(
            collective_id=0, has_side_effects=True, vmem_limit_bytes=62 * 1024 * 1024
        ),
    )(counts, bits, displacement, velocity, damage, broken)


def solution(mesh):
    return jax.shard_map(
        on_device,
        mesh=mesh,
        in_specs=(
            P(None, "slab", "col", None),
            P(None, "slab", "col", None),
            P("slab", "col", None),
            P(None, "slab", "col", None),
            P(),
            P(),
        ),
        out_specs=P(None, "slab", "col", None),
        check_vma=False,
    )
```

```python
import functools
import math

import jax
import jax.numpy as jnp
from jax import lax
from jax.experimental import pallas as pl
from jax.experimental.pallas import tpu as pltpu
from jax.sharding import PartitionSpec as P

MESH = pl.DeviceIdType.MESH
PLACE = (0, 2, 3)
BAND = 16
ROUNDS = 4
PIPES = 4
PARTS = 4


def bond_table():
    table = []
    for step_x in range(-2, 3):
        for step_y in range(-2, 3):
            for step_z in range(-2, 3):
                square = step_x * step_x + step_y * step_y + step_z * step_z
                if 0 < square <= 4 and (step_x, step_y, step_z) > (0, 0, 0):
                    length = math.sqrt(square)
                    table.append((step_x, step_y, step_z, (1.0 - length / 2.5) / length**3))
    return table


def moved_along_cells(value, step):
    cells = value.shape[-1]
    lane = lax.broadcasted_iota(jnp.int32, value.shape, value.ndim - 1)
    turned = pltpu.roll(value, (-step) % cells, value.ndim - 1)
    inside = (lane < cells - step) if step > 0 else (lane >= -step)
    return jnp.where(inside, turned, jnp.zeros_like(turned))


def kernel(
    counts, bits, displacement, velocity_in, damage, broken, result,
    fields, flags, velocity, fields_low, fields_high, flags_low, flags_high,
    rows_low, rows_high, row_flags_low, row_flags_high, far_low, far_high, far_flags,
    partial, back, returned, stage, arrived, ready_velocity, *rest,
):
    buffers, rest = rest[: 4 * PIPES], rest[4 * PIPES :]
    (
        col_send, col_recv, down_send, down_recv, back_send, back_recv,
        ride_send, ride_recv, load_done,
    ) = rest
    planes, rows, cells = damage.shape
    half = cells // 2
    slabs = lax.axis_size("slab")
    slab = lax.axis_index("slab")
    col = lax.axis_index("col")
    other = 1 - col
    has_low = slab > 0
    has_high = slab < slabs - 1
    table = bond_table()
    incoming = [buffers[2 * pipe : 2 * pipe + 2] for pipe in range(PIPES)]
    outgoing = [buffers[2 * (PIPES + pipe) : 2 * (PIPES + pipe) + 2] for pipe in range(PIPES)]

    inner = pl.ds(8, rows)
    loads = [
        pltpu.make_async_copy(
            displacement.at[component], fields.at[PLACE[component], 0:planes, inner],
            load_done.at[component],
        )
        for component in range(3)
    ]
    loads.append(
        pltpu.make_async_copy(damage, fields.at[1, 0:planes, inner], load_done.at[3])
    )
    load_flags = pltpu.make_async_copy(broken, flags.at[:, :, inner], load_done.at[4])
    load_velocity = pltpu.make_async_copy(velocity_in, velocity, load_done.at[5])
    for copy in loads + [load_flags, load_velocity]:
        copy.start()
    fields[:, 0:planes, 0:8] = jnp.zeros((4, planes, 8, cells), jnp.float32)
    fields[:, 0:planes, 8 + rows : 16 + rows] = jnp.zeros((4, planes, 8, cells), jnp.float32)
    fields[:, planes : planes + 2] = jnp.zeros((4, 2, rows + 16, cells), jnp.float32)
    flags[:, :, 0:8] = jnp.zeros((2, planes, 8, cells), jnp.int32)
    flags[:, :, 8 + rows : 16 + rows] = jnp.zeros((2, planes, 8, cells), jnp.int32)
    returned[...] = jnp.zeros_like(returned)
    stage[...] = jnp.zeros_like(stage)

    partners = []
    for bit in range(ROUNDS):
        weight = 1 << bit
        partners.append(slab + weight - 2 * weight * ((slab // weight) % 2))

    taken, rounds_of = [], []
    for number in range(ROUNDS):
        partner = partners[0]
        for bit in range(1, ROUNDS):
            partner = jnp.where(bits[number] == bit, partners[bit], partner)
        taken.append(jnp.minimum(counts[number, slab], counts[number, partner]))
    for bit in range(ROUNDS):
        place = jnp.int32(0)
        for number in range(1, ROUNDS):
            place = jnp.where(bits[number] == bit, number, place)
        rounds_of.append(place)

    barrier = pltpu.get_barrier_semaphore()

    def greet(to_slab, to_col):
        pl.semaphore_signal(barrier, inc=1, device_id=(to_slab, to_col), device_id_type=MESH)

    greet(slab, other)
    for partner in partners:
        greet(partner, col)

    @pl.when(has_low)
    def _():
        greet(slab - 1, col)
        greet(slab - 1, other)

    @pl.when(has_high)
    def _():
        greet(slab + 1, col)
        greet(slab + 1, other)

    sides = has_low.astype(jnp.int32) + has_high.astype(jnp.int32)
    pl.semaphore_wait(barrier, 1 + ROUNDS + 2 * sides)

    rim = pl.ds(pl.multiple_of(8 + (1 - col) * (rows - 8), 8), 8)
    ghost = pl.ds(pl.multiple_of((8 + rows) * col, 8), 8)

    def remote(source, target, sends, receives, to_slab, to_col):
        return pltpu.make_async_remote_copy(
            src_ref=source, dst_ref=target, send_sem=sends, recv_sem=receives,
            device_id=(to_slab, to_col), device_id_type=MESH,
        )

    beside = [
        remote(fields.at[:, 0:planes, rim], fields.at[:, 0:planes, ghost],
               col_send.at[0], col_recv.at[0], slab, other),
        remote(flags.at[:, :, rim], flags.at[:, :, ghost],
               col_send.at[1], col_recv.at[1], slab, other),
    ]
    below = [
        remote(fields.at[:, 0, inner], fields.at[:, planes, inner],
               down_send.at[0], down_recv.at[0], slab - 1, col),
        remote(fields.at[:, 0, rim], fields.at[:, planes, ghost],
               down_send.at[1], down_recv.at[1], slab - 1, other),
        remote(fields.at[0:2, 1, inner], fields.at[0:2, planes + 1, inner],
               down_send.at[2], down_recv.at[2], slab - 1, col),
    ]
    above = [
        remote(back.at[0:3], returned.at[0:3], back_send.at[0], back_recv.at[0], slab + 1, col),
        remote(back.at[3], returned.at[3], back_send.at[1], back_recv.at[1], slab + 1, col),
    ]

    for copy in loads:
        copy.wait()

    @pl.when(has_low)
    def _():
        for copy in below[0:2]:
            copy.start()

    beside[0].start()
    load_flags.wait()
    beside[1].start()

    column = lax.broadcasted_iota(jnp.int32, (3, 8, half), 1)

    def rides(pipe, step):
        parity = step % 2
        return [
            remote(outgoing[pipe][parity].at[bit], incoming[pipe][parity].at[bit],
                   ride_send.at[pipe, parity, bit], ride_recv.at[pipe, parity, bit],
                   partners[bit], col)
            for bit in range(ROUNDS)
        ]

    last = 2 * PARTS + ROUNDS - 1

    def ride(pipe, step):
        def spot(item):
            part = item % PARTS
            first = pipe * (rows // PIPES) + (part // 2) * 8
            return slice(first, first + 8), slice(part % 2 * half, (part % 2 + 1) * half)

        if step > 0:
            for copy in rides(pipe, step - 1):
                copy.wait_recv()
            source = incoming[pipe][(step - 1) % 2]
            for number in reversed(range(ROUNDS)):
                item = step - 1 - number
                if not 0 <= item < 2 * PARTS:
                    continue
                where, lanes = spot(item)
                new = jnp.where(
                    column < taken[number] - where.start,
                    source[bits[number]], stage[pipe, number],
                )
                if number < ROUNDS - 1:
                    stage[pipe, number + 1] = new
                elif item < PARTS:
                    arrived[:, where, lanes] = new
                else:
                    result[3:6, 0, where, lanes] = new
                    result[0:3, 0, where, lanes] = arrived[:, where, lanes] + 0.1 * new
        if step < last:
            if step < 2 * PARTS:
                where, lanes = spot(step)
                if step < PARTS:
                    tall = slice(where.start + 8, where.stop + 8)
                    for component in range(3):
                        stage[pipe, 0, component] = fields[PLACE[component], 0, tall, lanes]
                else:
                    stage[pipe, 0] = ready_velocity[:, where, lanes]
            if step >= 2:
                for copy in rides(pipe, step - 2):
                    copy.wait_send()
            target = outgoing[pipe][step % 2]
            for bit in range(ROUNDS):
                target[bit] = stage[pipe, rounds_of[bit]]
            for copy in rides(pipe, step):
                copy.start()
        else:
            for back_step in (last - 2, last - 1):
                for copy in rides(pipe, back_step):
                    copy.wait_send()

    def ride_both(step):
        for pipe in range(PIPES):
            ride(pipe, step)

    def shift_plane(plane, with_flags):
        for field in range(4):
            value = fields[field, plane]
            fields_low[field, plane] = moved_along_cells(value, -1)
            fields_high[field, plane] = moved_along_cells(value, 1)
        if with_flags:
            for part in range(2):
                value = flags[part, plane]
                flags_low[part, plane] = moved_along_cells(value, -1)
                flags_high[part, plane] = moved_along_cells(value, 1)

        def field_rows(field, carry):
            for place, source in enumerate((fields_low, fields, fields_high)):
                rows_low[place, field, plane] = source[field, plane, 7 : 7 + rows]
                rows_high[place, field, plane] = source[field, plane, 9 : 9 + rows]
            return carry

        lax.fori_loop(0, 4, field_rows, 0)
        if with_flags:

            def flag_rows(part, carry):
                for place, source in enumerate((flags_low, flags, flags_high)):
                    row_flags_low[place, part, plane] = source[part, plane, 7 : 7 + rows]
                    row_flags_high[place, part, plane] = source[part, plane, 9 : 9 + rows]
                return carry

            lax.fori_loop(0, 2, flag_rows, 0)
            for field in range(2):
                far_low[field, plane] = fields[field + 1, plane, 6 : 6 + rows]
                far_high[field, plane] = fields[field + 1, plane, 10 : 10 + rows]
            far_flags[plane] = flags[0, plane, 6 : 6 + rows]

    def force_on(plane, choose, emit, first=0, stop=rows // BAND):
        def body(index, carry):
            start = pl.multiple_of(index * BAND, 8)
            own_rows = pl.ds(start + 8, BAND)
            own = [fields[field, plane, own_rows] for field in range(4)]
            force = [jnp.zeros((BAND, cells), jnp.float32) for _ in range(3)]
            for number, (step_x, step_y, step_z, weight) in enumerate(table):
                for sign in (1, -1):
                    if not choose(step_x, sign):
                        continue
                    step = (sign * step_x, sign * step_y, sign * step_z)
                    there = plane + step[0]

                    def load(plain, low, high, less, more, far_less, far_more, first):
                        if step[1] == -2:
                            return far_less(first, there)
                        if step[1] == 2:
                            return far_more(first, there)
                        if step[1] != 0:
                            shifted = less if step[1] < 0 else more
                            return shifted[step[2] + 1, first, there, pl.ds(start, BAND)]
                        if step[2] == 0:
                            return plain[first, there, own_rows]
                        if step[2] == 1:
                            return high[first, there, own_rows]
                        if step[2] == -1:
                            return low[first, there, own_rows]
                        return moved_along_cells(plain[first, there, own_rows], step[2])

                    def field_at(first):
                        return load(
                            fields, fields_low, fields_high, rows_low, rows_high,
                            lambda f, p: far_low[f - 1, p, pl.ds(start, BAND)],
                            lambda f, p: far_high[f - 1, p, pl.ds(start, BAND)],
                            first,
                        )

                    along = None
                    for component in range(3):
                        if step[component] == 0:
                            continue
                        part = field_at(PLACE[component])
                        part = part - own[PLACE[component]]
                        if step[component] < 0:
                            part = -part
                        along = part if along is None else along + part
                    size = 2.0 if max(abs(s) for s in step) == 2 else 1.0
                    scale = field_at(1)
                    if sign == 1:
                        source = flags[number // 8, plane, own_rows]
                    else:
                        source = load(
                            flags, flags_low, flags_high, row_flags_low, row_flags_high,
                            lambda f, p: far_flags[p, pl.ds(start, BAND)], None, number // 8,
                        )
                    factor = (weight * size * size) * scale * along
                    factor = jnp.where(
                        jnp.bitwise_and(source, 1 << (number % 8)) == 0, factor, 0.0
                    )
                    for component in range(3):
                        if step[component] > 0:
                            force[component] = force[component] + factor
                        elif step[component] < 0:
                            force[component] = force[component] - factor
            emit(pl.ds(start, BAND), [own[1] * total for total in force])
            return carry

        lax.fori_loop(first, stop, body, 0)

    def keep_partial(plane):
        def emit(where, force):
            for component in range(3):
                partial[plane, component, where] = force[component]
        return emit

    def finish(plane):
        def emit(where, force):
            for component in range(3):
                new = velocity[component, plane, where] + 0.1 * force[component]
                result[3 + component, plane, where] = new
                result[component, plane, where] = (
                    fields[PLACE[component], plane, pl.ds(where.start + 8, BAND)] + 0.1 * new
                )
        return emit

    def keep_back(where, force):
        for component in range(3):
            back[component, where] = force[component]

    def keep_far(where, force):
        back[3, where] = force[0]

    ride_both(0)
    for copy in beside:
        copy.wait()

    @pl.when(has_low)
    def _():
        below[2].start()

    ride_both(1)

    def shift_own(plane, carry):
        shift_plane(plane, True)
        return carry

    lax.fori_loop(0, planes, shift_own, 0)
    ride_both(2)
    force_on(0, lambda step_x, sign: sign == 1 or step_x == 0, keep_partial(0))

    @pl.when(has_high)
    def _():
        for copy in below[0:2]:
            copy.wait_recv()

    force_on(planes, lambda step_x, sign: sign == -1 and step_x > 0, keep_back)

    @pl.when(has_high)
    def _():
        above[0].start()
        below[2].wait_recv()

    force_on(planes + 1, lambda step_x, sign: sign == -1 and step_x == 2, keep_far)

    @pl.when(has_high)
    def _():
        above[1].start()

    ride_both(3)
    load_velocity.wait()
    force_on(1, lambda step_x, sign: sign == 1 or step_x <= 1, keep_partial(1))

    @pl.when(has_low)
    def _():
        above[0].wait_recv()

    for component in range(3):
        total = partial[0, component] + returned[component]
        ready_velocity[component] = velocity[component, 0] + 0.1 * total
    ride_both(4)

    @pl.when(has_low)
    def _():
        above[1].wait_recv()
        for copy in below:
            copy.wait_send()

    @pl.when(has_high)
    def _():
        for copy in above:
            copy.wait_send()

    for component in range(3):
        total = partial[1, component]
        if component == 0:
            total = total + returned[3]
        new = velocity[component, 1] + 0.1 * total
        result[3 + component, 1] = new
        result[component, 1] = fields[PLACE[component], 1, 8 : 8 + rows] + 0.1 * new
    ride_both(5)
    bands = rows // BAND
    step = 6
    for plane in range(2, planes):
        if plane == planes - 1:
            shift_plane(planes, False)
        for part in range(2):
            force_on(
                plane, lambda step_x, sign: True, finish(plane),
                part * bands // 2, (part + 1) * bands // 2,
            )
            ride_both(step)
            step += 1
    for step in range(step, last + 1):
        ride_both(step)


def on_device(displacement, velocity, damage, broken, counts, bits):
    planes, rows, cells = damage.shape
    half = cells // 2
    vmem = pl.BlockSpec(memory_space=pltpu.VMEM)
    smem = pl.BlockSpec(memory_space=pltpu.SMEM)
    hbm = pl.BlockSpec(memory_space=pltpu.HBM)
    f32, i32 = jnp.float32, jnp.int32
    tall = rows + 16
    return pl.pallas_call(
        kernel,
        out_shape=jax.ShapeDtypeStruct((6, planes, rows, cells), f32),
        in_specs=[smem] * 2 + [hbm] * 4,
        out_specs=vmem,
        scratch_shapes=[
            pltpu.VMEM((4, planes + 2, tall, cells), f32),
            pltpu.VMEM((2, planes, tall, cells), i32),
            pltpu.VMEM((3, planes, rows, cells), f32),
            pltpu.VMEM((4, planes + 1, tall, cells), f32),
            pltpu.VMEM((4, planes + 1, tall, cells), f32),
            pltpu.VMEM((2, planes, tall, cells), i32),
            pltpu.VMEM((2, planes, tall, cells), i32),
            pltpu.VMEM((3, 4, planes + 1, rows, cells), f32),
            pltpu.VMEM((3, 4, planes + 1, rows, cells), f32),
            pltpu.VMEM((3, 2, planes, rows, cells), i32),
            pltpu.VMEM((3, 2, planes, rows, cells), i32),
            pltpu.VMEM((2, planes, rows, cells), f32),
            pltpu.VMEM((2, planes, rows, cells), f32),
            pltpu.VMEM((planes, rows, cells), i32),
            pltpu.VMEM((2, 3, rows, cells), f32),
            pltpu.VMEM((4, rows, cells), f32),
            pltpu.VMEM((4, rows, cells), f32),
            pltpu.VMEM((PIPES, ROUNDS, 3, 8, half), f32),
            pltpu.VMEM((3, rows, cells), f32),
            pltpu.VMEM((3, rows, cells), f32),
        ]
        + [pltpu.VMEM((ROUNDS, 3, 8, half), f32)] * (4 * PIPES)
        + [
            pltpu.SemaphoreType.DMA((2,)),
            pltpu.SemaphoreType.DMA((2,)),
            pltpu.SemaphoreType.DMA((3,)),
            pltpu.SemaphoreType.DMA((3,)),
            pltpu.SemaphoreType.DMA((2,)),
            pltpu.SemaphoreType.DMA((2,)),
            pltpu.SemaphoreType.DMA((PIPES, 2, ROUNDS)),
            pltpu.SemaphoreType.DMA((PIPES, 2, ROUNDS)),
            pltpu.SemaphoreType.DMA((6,)),
        ],
        compiler_params=pltpu.CompilerParams(
            collective_id=0, has_side_effects=True, vmem_limit_bytes=60 * 1024 * 1024
        ),
    )(counts.T, bits, displacement, velocity, damage, broken)


def solution(mesh):
    return jax.shard_map(
        on_device,
        mesh=mesh,
        in_specs=(
            P(None, "slab", "col", None),
            P(None, "slab", "col", None),
            P("slab", "col", None),
            P(None, "slab", "col", None),
            P(),
            P(),
        ),
        out_specs=P(None, "slab", "col", None),
        check_vma=False,
    )
```

```python
import functools
import math

import jax
import jax.numpy as jnp
from jax import lax
from jax.experimental import pallas as pl
from jax.experimental.pallas import tpu as pltpu
from jax.sharding import PartitionSpec as P

MESH = pl.DeviceIdType.MESH
PLACE = (0, 2, 3)
BAND = 16
ROUNDS = 4
PIPES = 2
PARTS = 4


def bond_table():
    table = []
    for step_x in range(-2, 3):
        for step_y in range(-2, 3):
            for step_z in range(-2, 3):
                square = step_x * step_x + step_y * step_y + step_z * step_z
                if 0 < square <= 4 and (step_x, step_y, step_z) > (0, 0, 0):
                    length = math.sqrt(square)
                    table.append((step_x, step_y, step_z, (1.0 - length / 2.5) / length**3))
    return table


def moved_along_cells(value, step):
    cells = value.shape[-1]
    lane = lax.broadcasted_iota(jnp.int32, value.shape, value.ndim - 1)
    turned = pltpu.roll(value, (-step) % cells, value.ndim - 1)
    inside = (lane < cells - step) if step > 0 else (lane >= -step)
    return jnp.where(inside, turned, jnp.zeros_like(turned))


def kernel(
    counts, bits, displacement, velocity_in, damage, broken, result,
    fields, flags, velocity, fields_low, fields_high, flags_low, flags_high,
    rows_low, rows_high, row_flags_low, row_flags_high, far_low, far_high, far_flags,
    partial, back, returned, stage, arrived, ready_velocity, *rest,
):
    buffers, rest = rest[: 4 * PIPES], rest[4 * PIPES :]
    (
        col_send, col_recv, down_send, down_recv, back_send, back_recv,
        ride_send, ride_recv, load_done,
    ) = rest
    planes, rows, cells = damage.shape
    slabs = lax.axis_size("slab")
    slab = lax.axis_index("slab")
    col = lax.axis_index("col")
    other = 1 - col
    has_low = slab > 0
    has_high = slab < slabs - 1
    table = bond_table()
    incoming = [buffers[2 * pipe : 2 * pipe + 2] for pipe in range(PIPES)]
    outgoing = [buffers[2 * (PIPES + pipe) : 2 * (PIPES + pipe) + 2] for pipe in range(PIPES)]

    inner = pl.ds(8, rows)
    loads = [
        pltpu.make_async_copy(
            displacement.at[component], fields.at[PLACE[component], 0:planes, inner],
            load_done.at[component],
        )
        for component in range(3)
    ]
    loads.append(
        pltpu.make_async_copy(damage, fields.at[1, 0:planes, inner], load_done.at[3])
    )
    load_flags = pltpu.make_async_copy(broken, flags.at[:, :, inner], load_done.at[4])
    load_velocity = pltpu.make_async_copy(velocity_in, velocity, load_done.at[5])
    for copy in loads + [load_flags, load_velocity]:
        copy.start()
    fields[:, 0:planes, 0:8] = jnp.zeros((4, planes, 8, cells), jnp.float32)
    fields[:, 0:planes, 8 + rows : 16 + rows] = jnp.zeros((4, planes, 8, cells), jnp.float32)
    fields[:, planes : planes + 2] = jnp.zeros((4, 2, rows + 16, cells), jnp.float32)
    flags[:, :, 0:8] = jnp.zeros((2, planes, 8, cells), jnp.int32)
    flags[:, :, 8 + rows : 16 + rows] = jnp.zeros((2, planes, 8, cells), jnp.int32)
    returned[...] = jnp.zeros_like(returned)
    stage[...] = jnp.zeros_like(stage)

    partners = []
    for bit in range(ROUNDS):
        weight = 1 << bit
        partners.append(slab + weight - 2 * weight * ((slab // weight) % 2))

    taken, rounds_of = [], []
    for number in range(ROUNDS):
        partner = partners[0]
        for bit in range(1, ROUNDS):
            partner = jnp.where(bits[number] == bit, partners[bit], partner)
        taken.append(jnp.minimum(counts[number, slab], counts[number, partner]))
    for bit in range(ROUNDS):
        place = jnp.int32(0)
        for number in range(1, ROUNDS):
            place = jnp.where(bits[number] == bit, number, place)
        rounds_of.append(place)

    barrier = pltpu.get_barrier_semaphore()

    def greet(to_slab, to_col):
        pl.semaphore_signal(barrier, inc=1, device_id=(to_slab, to_col), device_id_type=MESH)

    greet(slab, other)
    for partner in partners:
        greet(partner, col)

    @pl.when(has_low)
    def _():
        greet(slab - 1, col)
        greet(slab - 1, other)

    @pl.when(has_high)
    def _():
        greet(slab + 1, col)
        greet(slab + 1, other)

    sides = has_low.astype(jnp.int32) + has_high.astype(jnp.int32)
    pl.semaphore_wait(barrier, 1 + ROUNDS + 2 * sides)

    rim = pl.ds(pl.multiple_of(8 + (1 - col) * (rows - 8), 8), 8)
    ghost = pl.ds(pl.multiple_of((8 + rows) * col, 8), 8)

    def remote(source, target, sends, receives, to_slab, to_col):
        return pltpu.make_async_remote_copy(
            src_ref=source, dst_ref=target, send_sem=sends, recv_sem=receives,
            device_id=(to_slab, to_col), device_id_type=MESH,
        )

    beside = [
        remote(fields.at[:, 0:planes, rim], fields.at[:, 0:planes, ghost],
               col_send.at[0], col_recv.at[0], slab, other),
        remote(flags.at[:, :, rim], flags.at[:, :, ghost],
               col_send.at[1], col_recv.at[1], slab, other),
    ]
    below = [
        remote(fields.at[:, 0, inner], fields.at[:, planes, inner],
               down_send.at[0], down_recv.at[0], slab - 1, col),
        remote(fields.at[:, 0, rim], fields.at[:, planes, ghost],
               down_send.at[1], down_recv.at[1], slab - 1, other),
        remote(fields.at[0:2, 1, inner], fields.at[0:2, planes + 1, inner],
               down_send.at[2], down_recv.at[2], slab - 1, col),
    ]
    above = [
        remote(back.at[0:3], returned.at[0:3], back_send.at[0], back_recv.at[0], slab + 1, col),
        remote(back.at[3], returned.at[3], back_send.at[1], back_recv.at[1], slab + 1, col),
    ]

    for copy in loads:
        copy.wait()

    @pl.when(has_low)
    def _():
        for copy in below[0:2]:
            copy.start()

    beside[0].start()
    load_flags.wait()
    beside[1].start()

    column = lax.broadcasted_iota(jnp.int32, (3, 8, cells), 1)

    def rides(pipe, step):
        parity = step % 2
        return [
            remote(outgoing[pipe][parity].at[bit], incoming[pipe][parity].at[bit],
                   ride_send.at[pipe, parity, bit], ride_recv.at[pipe, parity, bit],
                   partners[bit], col)
            for bit in range(ROUNDS)
        ]

    last = 2 * PARTS + ROUNDS - 1

    def ride(pipe, step):
        def spot(item):
            part = item % PARTS
            first = pipe * (rows // PIPES) + part * 8
            return slice(first, first + 8), slice(0, cells)

        if step > 0:
            for copy in rides(pipe, step - 1):
                copy.wait_recv()
            source = incoming[pipe][(step - 1) % 2]
            for number in reversed(range(ROUNDS)):
                item = step - 1 - number
                if not 0 <= item < 2 * PARTS:
                    continue
                where, lanes = spot(item)
                new = jnp.where(
                    column < taken[number] - where.start,
                    source[bits[number]], stage[pipe, number],
                )
                if number < ROUNDS - 1:
                    stage[pipe, number + 1] = new
                elif item < PARTS:
                    arrived[:, where, lanes] = new
                else:
                    result[3:6, 0, where, lanes] = new
                    result[0:3, 0, where, lanes] = arrived[:, where, lanes] + 0.1 * new
        if step < last:
            if step < 2 * PARTS:
                where, lanes = spot(step)
                if step < PARTS:
                    tall = slice(where.start + 8, where.stop + 8)
                    for component in range(3):
                        stage[pipe, 0, component] = fields[PLACE[component], 0, tall, lanes]
                else:
                    stage[pipe, 0] = ready_velocity[:, where, lanes]
            if step >= 2:
                for copy in rides(pipe, step - 2):
                    copy.wait_send()
            target = outgoing[pipe][step % 2]
            for bit in range(ROUNDS):
                target[bit] = stage[pipe, rounds_of[bit]]
            for copy in rides(pipe, step):
                copy.start()
        else:
            for back_step in (last - 2, last - 1):
                for copy in rides(pipe, back_step):
                    copy.wait_send()

    def ride_both(step):
        for pipe in range(PIPES):
            ride(pipe, step)

    def shift_plane(plane, with_flags):
        for field in range(4):
            value = fields[field, plane]
            fields_low[field, plane] = moved_along_cells(value, -1)
            fields_high[field, plane] = moved_along_cells(value, 1)
        if with_flags:
            for part in range(2):
                value = flags[part, plane]
                flags_low[part, plane] = moved_along_cells(value, -1)
                flags_high[part, plane] = moved_along_cells(value, 1)

        def field_rows(field, carry):
            for place, source in enumerate((fields_low, fields, fields_high)):
                rows_low[place, field, plane] = source[field, plane, 7 : 7 + rows]
                rows_high[place, field, plane] = source[field, plane, 9 : 9 + rows]
            return carry

        lax.fori_loop(0, 4, field_rows, 0)
        if with_flags:

            def flag_rows(part, carry):
                for place, source in enumerate((flags_low, flags, flags_high)):
                    row_flags_low[place, part, plane] = source[part, plane, 7 : 7 + rows]
                    row_flags_high[place, part, plane] = source[part, plane, 9 : 9 + rows]
                return carry

            lax.fori_loop(0, 2, flag_rows, 0)
            for field in range(2):
                far_low[field, plane] = fields[field + 1, plane, 6 : 6 + rows]
                far_high[field, plane] = fields[field + 1, plane, 10 : 10 + rows]
            far_flags[plane] = flags[0, plane, 6 : 6 + rows]

    def force_on(plane, choose, emit, first=0, stop=rows // BAND):
        def body(index, carry):
            start = pl.multiple_of(index * BAND, 8)
            own_rows = pl.ds(start + 8, BAND)
            own = [fields[field, plane, own_rows] for field in range(4)]
            force = [jnp.zeros((BAND, cells), jnp.float32) for _ in range(3)]
            for number, (step_x, step_y, step_z, weight) in enumerate(table):
                for sign in (1, -1):
                    if not choose(step_x, sign):
                        continue
                    step = (sign * step_x, sign * step_y, sign * step_z)
                    there = plane + step[0]

                    def load(plain, low, high, less, more, far_less, far_more, first):
                        if step[1] == -2:
                            return far_less(first, there)
                        if step[1] == 2:
                            return far_more(first, there)
                        if step[1] != 0:
                            shifted = less if step[1] < 0 else more
                            return shifted[step[2] + 1, first, there, pl.ds(start, BAND)]
                        if step[2] == 0:
                            return plain[first, there, own_rows]
                        if step[2] == 1:
                            return high[first, there, own_rows]
                        if step[2] == -1:
                            return low[first, there, own_rows]
                        return moved_along_cells(plain[first, there, own_rows], step[2])

                    def field_at(first):
                        return load(
                            fields, fields_low, fields_high, rows_low, rows_high,
                            lambda f, p: far_low[f - 1, p, pl.ds(start, BAND)],
                            lambda f, p: far_high[f - 1, p, pl.ds(start, BAND)],
                            first,
                        )

                    along = None
                    for component in range(3):
                        if step[component] == 0:
                            continue
                        part = field_at(PLACE[component])
                        part = part - own[PLACE[component]]
                        if step[component] < 0:
                            part = -part
                        along = part if along is None else along + part
                    size = 2.0 if max(abs(s) for s in step) == 2 else 1.0
                    scale = field_at(1)
                    if sign == 1:
                        source = flags[number // 8, plane, own_rows]
                    else:
                        source = load(
                            flags, flags_low, flags_high, row_flags_low, row_flags_high,
                            lambda f, p: far_flags[p, pl.ds(start, BAND)], None, number // 8,
                        )
                    factor = (weight * size * size) * scale * along
                    factor = jnp.where(
                        jnp.bitwise_and(source, 1 << (number % 8)) == 0, factor, 0.0
                    )
                    for component in range(3):
                        if step[component] > 0:
                            force[component] = force[component] + factor
                        elif step[component] < 0:
                            force[component] = force[component] - factor
            emit(pl.ds(start, BAND), [own[1] * total for total in force])
            return carry

        lax.fori_loop(first, stop, body, 0)

    def keep_partial(plane):
        def emit(where, force):
            for component in range(3):
                partial[plane, component, where] = force[component]
        return emit

    def finish(plane):
        def emit(where, force):
            for component in range(3):
                new = velocity[component, plane, where] + 0.1 * force[component]
                result[3 + component, plane, where] = new
                result[component, plane, where] = (
                    fields[PLACE[component], plane, pl.ds(where.start + 8, BAND)] + 0.1 * new
                )
        return emit

    def keep_back(where, force):
        for component in range(3):
            back[component, where] = force[component]

    def keep_far(where, force):
        back[3, where] = force[0]

    ride_both(0)
    for copy in beside:
        copy.wait()

    @pl.when(has_low)
    def _():
        below[2].start()

    ride_both(1)

    def shift_own(plane, carry):
        shift_plane(plane, True)
        return carry

    lax.fori_loop(0, planes, shift_own, 0)
    ride_both(2)
    force_on(0, lambda step_x, sign: sign == 1 or step_x == 0, keep_partial(0))

    @pl.when(has_high)
    def _():
        for copy in below[0:2]:
            copy.wait_recv()

    force_on(planes, lambda step_x, sign: sign == -1 and step_x > 0, keep_back)

    @pl.when(has_high)
    def _():
        above[0].start()
        below[2].wait_recv()

    force_on(planes + 1, lambda step_x, sign: sign == -1 and step_x == 2, keep_far)

    @pl.when(has_high)
    def _():
        above[1].start()

    ride_both(3)
    load_velocity.wait()
    force_on(1, lambda step_x, sign: sign == 1 or step_x <= 1, keep_partial(1))

    @pl.when(has_low)
    def _():
        above[0].wait_recv()

    for component in range(3):
        total = partial[0, component] + returned[component]
        ready_velocity[component] = velocity[component, 0] + 0.1 * total
    ride_both(4)

    @pl.when(has_low)
    def _():
        above[1].wait_recv()
        for copy in below:
            copy.wait_send()

    @pl.when(has_high)
    def _():
        for copy in above:
            copy.wait_send()

    for component in range(3):
        total = partial[1, component]
        if component == 0:
            total = total + returned[3]
        new = velocity[component, 1] + 0.1 * total
        result[3 + component, 1] = new
        result[component, 1] = fields[PLACE[component], 1, 8 : 8 + rows] + 0.1 * new
    ride_both(5)
    bands = rows // BAND
    step = 6
    for plane in range(2, planes):
        if plane == planes - 1:
            shift_plane(planes, False)
        for part in range(2):
            force_on(
                plane, lambda step_x, sign: True, finish(plane),
                part * bands // 2, (part + 1) * bands // 2,
            )
            ride_both(step)
            step += 1
    for step in range(step, last + 1):
        ride_both(step)


def on_device(displacement, velocity, damage, broken, counts, bits):
    planes, rows, cells = damage.shape
    vmem = pl.BlockSpec(memory_space=pltpu.VMEM)
    smem = pl.BlockSpec(memory_space=pltpu.SMEM)
    hbm = pl.BlockSpec(memory_space=pltpu.HBM)
    f32, i32 = jnp.float32, jnp.int32
    tall = rows + 16
    return pl.pallas_call(
        kernel,
        out_shape=jax.ShapeDtypeStruct((6, planes, rows, cells), f32),
        in_specs=[smem] * 2 + [hbm] * 4,
        out_specs=vmem,
        scratch_shapes=[
            pltpu.VMEM((4, planes + 2, tall, cells), f32),
            pltpu.VMEM((2, planes, tall, cells), i32),
            pltpu.VMEM((3, planes, rows, cells), f32),
            pltpu.VMEM((4, planes + 1, tall, cells), f32),
            pltpu.VMEM((4, planes + 1, tall, cells), f32),
            pltpu.VMEM((2, planes, tall, cells), i32),
            pltpu.VMEM((2, planes, tall, cells), i32),
            pltpu.VMEM((3, 4, planes + 1, rows, cells), f32),
            pltpu.VMEM((3, 4, planes + 1, rows, cells), f32),
            pltpu.VMEM((3, 2, planes, rows, cells), i32),
            pltpu.VMEM((3, 2, planes, rows, cells), i32),
            pltpu.VMEM((2, planes, rows, cells), f32),
            pltpu.VMEM((2, planes, rows, cells), f32),
            pltpu.VMEM((planes, rows, cells), i32),
            pltpu.VMEM((2, 3, rows, cells), f32),
            pltpu.VMEM((4, rows, cells), f32),
            pltpu.VMEM((4, rows, cells), f32),
            pltpu.VMEM((PIPES, ROUNDS, 3, 8, cells), f32),
            pltpu.VMEM((3, rows, cells), f32),
            pltpu.VMEM((3, rows, cells), f32),
        ]
        + [pltpu.VMEM((ROUNDS, 3, 8, cells), f32)] * (4 * PIPES)
        + [
            pltpu.SemaphoreType.DMA((2,)),
            pltpu.SemaphoreType.DMA((2,)),
            pltpu.SemaphoreType.DMA((3,)),
            pltpu.SemaphoreType.DMA((3,)),
            pltpu.SemaphoreType.DMA((2,)),
            pltpu.SemaphoreType.DMA((2,)),
            pltpu.SemaphoreType.DMA((PIPES, 2, ROUNDS)),
            pltpu.SemaphoreType.DMA((PIPES, 2, ROUNDS)),
            pltpu.SemaphoreType.DMA((6,)),
        ],
        compiler_params=pltpu.CompilerParams(
            collective_id=0, has_side_effects=True, vmem_limit_bytes=60 * 1024 * 1024
        ),
    )(counts.T, bits, displacement, velocity, damage, broken)


def solution(mesh):
    return jax.shard_map(
        on_device,
        mesh=mesh,
        in_specs=(
            P(None, "slab", "col", None),
            P(None, "slab", "col", None),
            P("slab", "col", None),
            P(None, "slab", "col", None),
            P(),
            P(),
        ),
        out_specs=P(None, "slab", "col", None),
        check_vma=False,
    )
```

```python
import functools
import math

import jax
import jax.numpy as jnp
from jax import lax
from jax.experimental import pallas as pl
from jax.experimental.pallas import tpu as pltpu
from jax.sharding import PartitionSpec as P

MESH = pl.DeviceIdType.MESH
PLACE = (0, 2, 3)
BAND = 16
ROUNDS = 4
PIPES = 4
PARTS = 4


def bond_table():
    table = []
    for step_x in range(-2, 3):
        for step_y in range(-2, 3):
            for step_z in range(-2, 3):
                square = step_x * step_x + step_y * step_y + step_z * step_z
                if 0 < square <= 4 and (step_x, step_y, step_z) > (0, 0, 0):
                    length = math.sqrt(square)
                    table.append((step_x, step_y, step_z, (1.0 - length / 2.5) / length**3))
    return table


def moved_along_cells(value, step):
    cells = value.shape[-1]
    lane = lax.broadcasted_iota(jnp.int32, value.shape, value.ndim - 1)
    turned = pltpu.roll(value, (-step) % cells, value.ndim - 1)
    inside = (lane < cells - step) if step > 0 else (lane >= -step)
    return jnp.where(inside, turned, jnp.zeros_like(turned))


def kernel(
    counts, bits, displacement, velocity_in, damage, broken, result,
    fields, flags, velocity, fields_low, fields_high, flags_low, flags_high,
    rows_low, rows_high, row_flags_low, row_flags_high, far_low, far_high, far_flags,
    partial, back, returned, stage, arrived, ready_velocity, *rest,
):
    buffers, rest = rest[: 4 * PIPES], rest[4 * PIPES :]
    (
        col_send, col_recv, down_send, down_recv, back_send, back_recv,
        ride_send, ride_recv, load_done,
    ) = rest
    planes, rows, cells = damage.shape
    half = cells // 2
    slabs = lax.axis_size("slab")
    slab = lax.axis_index("slab")
    col = lax.axis_index("col")
    other = 1 - col
    has_low = slab > 0
    has_high = slab < slabs - 1
    table = bond_table()
    incoming = [buffers[2 * pipe : 2 * pipe + 2] for pipe in range(PIPES)]
    outgoing = [buffers[2 * (PIPES + pipe) : 2 * (PIPES + pipe) + 2] for pipe in range(PIPES)]

    inner = pl.ds(8, rows)
    loads = [
        pltpu.make_async_copy(
            displacement.at[component], fields.at[PLACE[component], 0:planes, inner],
            load_done.at[component],
        )
        for component in range(3)
    ]
    loads.append(
        pltpu.make_async_copy(damage, fields.at[1, 0:planes, inner], load_done.at[3])
    )
    load_flags = pltpu.make_async_copy(broken, flags.at[:, :, inner], load_done.at[4])
    load_velocity = pltpu.make_async_copy(velocity_in, velocity, load_done.at[5])
    for copy in loads + [load_flags, load_velocity]:
        copy.start()
    fields[:, 0:planes, 0:8] = jnp.zeros((4, planes, 8, cells), jnp.float32)
    fields[:, 0:planes, 8 + rows : 16 + rows] = jnp.zeros((4, planes, 8, cells), jnp.float32)
    fields[:, planes : planes + 2] = jnp.zeros((4, 2, rows + 16, cells), jnp.float32)
    flags[:, :, 0:8] = jnp.zeros((2, planes, 8, cells), jnp.int32)
    flags[:, :, 8 + rows : 16 + rows] = jnp.zeros((2, planes, 8, cells), jnp.int32)
    returned[...] = jnp.zeros_like(returned)
    stage[...] = jnp.zeros_like(stage)

    partners = []
    for bit in range(ROUNDS):
        weight = 1 << bit
        partners.append(slab + weight - 2 * weight * ((slab // weight) % 2))

    taken, rounds_of = [], []
    for number in range(ROUNDS):
        partner = partners[0]
        for bit in range(1, ROUNDS):
            partner = jnp.where(bits[number] == bit, partners[bit], partner)
        taken.append(jnp.minimum(counts[number, slab], counts[number, partner]))
    for bit in range(ROUNDS):
        place = jnp.int32(0)
        for number in range(1, ROUNDS):
            place = jnp.where(bits[number] == bit, number, place)
        rounds_of.append(place)

    barrier = pltpu.get_barrier_semaphore()

    def greet(to_slab, to_col):
        pl.semaphore_signal(barrier, inc=1, device_id=(to_slab, to_col), device_id_type=MESH)

    greet(slab, other)
    for partner in partners:
        greet(partner, col)

    @pl.when(has_low)
    def _():
        greet(slab - 1, col)
        greet(slab - 1, other)

    @pl.when(has_high)
    def _():
        greet(slab + 1, col)
        greet(slab + 1, other)

    sides = has_low.astype(jnp.int32) + has_high.astype(jnp.int32)
    pl.semaphore_wait(barrier, 1 + ROUNDS + 2 * sides)

    rim = pl.ds(pl.multiple_of(8 + (1 - col) * (rows - 8), 8), 8)
    ghost = pl.ds(pl.multiple_of((8 + rows) * col, 8), 8)

    def remote(source, target, sends, receives, to_slab, to_col):
        return pltpu.make_async_remote_copy(
            src_ref=source, dst_ref=target, send_sem=sends, recv_sem=receives,
            device_id=(to_slab, to_col), device_id_type=MESH,
        )

    beside = [
        remote(fields.at[:, 0:planes, rim], fields.at[:, 0:planes, ghost],
               col_send.at[0], col_recv.at[0], slab, other),
        remote(flags.at[:, :, rim], flags.at[:, :, ghost],
               col_send.at[1], col_recv.at[1], slab, other),
    ]
    below = [
        remote(fields.at[:, 0, inner], fields.at[:, planes, inner],
               down_send.at[0], down_recv.at[0], slab - 1, col),
        remote(fields.at[:, 0, rim], fields.at[:, planes, ghost],
               down_send.at[1], down_recv.at[1], slab - 1, other),
        remote(fields.at[0:2, 1, inner], fields.at[0:2, planes + 1, inner],
               down_send.at[2], down_recv.at[2], slab - 1, col),
    ]
    above = [
        remote(back.at[0:3], returned.at[0:3], back_send.at[0], back_recv.at[0], slab + 1, col),
        remote(back.at[3], returned.at[3], back_send.at[1], back_recv.at[1], slab + 1, col),
    ]

    for copy in loads:
        copy.wait()

    @pl.when(has_low)
    def _():
        for copy in below[0:2]:
            copy.start()

    beside[0].start()
    load_flags.wait()
    beside[1].start()

    column = lax.broadcasted_iota(jnp.int32, (3, 8, half), 1)

    def rides(pipe, step):
        parity = step % 2
        return [
            remote(outgoing[pipe][parity].at[bit], incoming[pipe][parity].at[bit],
                   ride_send.at[pipe, parity, bit], ride_recv.at[pipe, parity, bit],
                   partners[bit], col)
            for bit in range(ROUNDS)
        ]

    last = 2 * PARTS + ROUNDS - 1

    def ride(pipe, step):
        def spot(item):
            part = item % PARTS
            first = pipe * (rows // PIPES) + (part // 2) * 8
            return slice(first, first + 8), slice(part % 2 * half, (part % 2 + 1) * half)

        if step > 0:
            for copy in rides(pipe, step - 1):
                copy.wait_recv()
            source = incoming[pipe][(step - 1) % 2]
            for number in reversed(range(ROUNDS)):
                item = step - 1 - number
                if not 0 <= item < 2 * PARTS:
                    continue
                where, lanes = spot(item)
                new = jnp.where(
                    column < taken[number] - where.start,
                    source[bits[number]], stage[pipe, number],
                )
                if number < ROUNDS - 1:
                    stage[pipe, number + 1] = new
                elif item < PARTS:
                    arrived[:, where, lanes] = new
                else:
                    result[3:6, 0, where, lanes] = new
                    result[0:3, 0, where, lanes] = arrived[:, where, lanes] + 0.1 * new
        if step < last:
            if step < 2 * PARTS:
                where, lanes = spot(step)
                if step < PARTS:
                    tall = slice(where.start + 8, where.stop + 8)
                    for component in range(3):
                        stage[pipe, 0, component] = fields[PLACE[component], 0, tall, lanes]
                else:
                    stage[pipe, 0] = ready_velocity[:, where, lanes]
            if step >= 2:
                for copy in rides(pipe, step - 2):
                    copy.wait_send()
            target = outgoing[pipe][step % 2]
            for bit in range(ROUNDS):
                target[bit] = stage[pipe, rounds_of[bit]]
            for copy in rides(pipe, step):
                copy.start()
        else:
            for back_step in (last - 2, last - 1):
                for copy in rides(pipe, back_step):
                    copy.wait_send()

    def ride_both(step):
        for pipe in range(PIPES):
            ride(pipe, step)

    def shift_plane(plane, with_flags):
        for field in range(4):
            value = fields[field, plane]
            fields_low[field, plane] = moved_along_cells(value, -1)
            fields_high[field, plane] = moved_along_cells(value, 1)
        if with_flags:
            for part in range(2):
                value = flags[part, plane]
                flags_low[part, plane] = moved_along_cells(value, -1)
                flags_high[part, plane] = moved_along_cells(value, 1)

        def field_rows(field, carry):
            for place, source in enumerate((fields_low, fields, fields_high)):
                rows_low[place, field, plane] = source[field, plane, 7 : 7 + rows]
                rows_high[place, field, plane] = source[field, plane, 9 : 9 + rows]
            return carry

        lax.fori_loop(0, 4, field_rows, 0)
        if with_flags:

            def flag_rows(part, carry):
                for place, source in enumerate((flags_low, flags, flags_high)):
                    row_flags_low[place, part, plane] = source[part, plane, 7 : 7 + rows]
                    row_flags_high[place, part, plane] = source[part, plane, 9 : 9 + rows]
                return carry

            lax.fori_loop(0, 2, flag_rows, 0)
            for field in range(2):
                far_low[field, plane] = fields[field + 1, plane, 6 : 6 + rows]
                far_high[field, plane] = fields[field + 1, plane, 10 : 10 + rows]
            far_flags[plane] = flags[0, plane, 6 : 6 + rows]

    def force_on(plane, choose, emit, first=0, stop=rows // BAND):
        def body(index, carry):
            start = pl.multiple_of(index * BAND, 8)
            own_rows = pl.ds(start + 8, BAND)
            own = [fields[field, plane, own_rows] for field in range(4)]
            force = [jnp.zeros((BAND, cells), jnp.float32) for _ in range(3)]
            for number, (step_x, step_y, step_z, weight) in enumerate(table):
                for sign in (1, -1):
                    if not choose(step_x, sign):
                        continue
                    step = (sign * step_x, sign * step_y, sign * step_z)
                    there = plane + step[0]

                    def load(plain, low, high, less, more, far_less, far_more, first):
                        if step[1] == -2:
                            return far_less(first, there)
                        if step[1] == 2:
                            return far_more(first, there)
                        if step[1] != 0:
                            shifted = less if step[1] < 0 else more
                            return shifted[step[2] + 1, first, there, pl.ds(start, BAND)]
                        if step[2] == 0:
                            return plain[first, there, own_rows]
                        if step[2] == 1:
                            return high[first, there, own_rows]
                        if step[2] == -1:
                            return low[first, there, own_rows]
                        return moved_along_cells(plain[first, there, own_rows], step[2])

                    def field_at(first):
                        return load(
                            fields, fields_low, fields_high, rows_low, rows_high,
                            lambda f, p: far_low[f - 1, p, pl.ds(start, BAND)],
                            lambda f, p: far_high[f - 1, p, pl.ds(start, BAND)],
                            first,
                        )

                    along = None
                    for component in range(3):
                        if step[component] == 0:
                            continue
                        part = field_at(PLACE[component])
                        part = part - own[PLACE[component]]
                        if step[component] < 0:
                            part = -part
                        along = part if along is None else along + part
                    size = 2.0 if max(abs(s) for s in step) == 2 else 1.0
                    scale = field_at(1)
                    if sign == 1:
                        source = flags[number // 8, plane, own_rows]
                    else:
                        source = load(
                            flags, flags_low, flags_high, row_flags_low, row_flags_high,
                            lambda f, p: far_flags[p, pl.ds(start, BAND)], None, number // 8,
                        )
                    factor = (weight * size * size) * scale * along
                    factor = jnp.where(
                        jnp.bitwise_and(source, 1 << (number % 8)) == 0, factor, 0.0
                    )
                    for component in range(3):
                        if step[component] > 0:
                            force[component] = force[component] + factor
                        elif step[component] < 0:
                            force[component] = force[component] - factor
            emit(pl.ds(start, BAND), [own[1] * total for total in force])
            return carry

        lax.fori_loop(first, stop, body, 0)

    def keep_partial(plane):
        def emit(where, force):
            for component in range(3):
                partial[plane, component, where] = force[component]
        return emit

    def finish(plane):
        def emit(where, force):
            for component in range(3):
                new = velocity[component, plane, where] + 0.1 * force[component]
                result[3 + component, plane, where] = new
                result[component, plane, where] = (
                    fields[PLACE[component], plane, pl.ds(where.start + 8, BAND)] + 0.1 * new
                )
        return emit

    def keep_back(where, force):
        for component in range(3):
            back[component, where] = force[component]

    def keep_far(where, force):
        back[3, where] = force[0]

    ride_both(0)
    for copy in beside:
        copy.wait()

    @pl.when(has_low)
    def _():
        below[2].start()

    ride_both(1)

    def shift_own(plane, carry):
        shift_plane(plane, True)
        return carry

    lax.fori_loop(0, planes, shift_own, 0)
    ride_both(2)
    force_on(0, lambda step_x, sign: sign == 1 or step_x == 0, keep_partial(0))

    @pl.when(has_high)
    def _():
        for copy in below[0:2]:
            copy.wait_recv()

    force_on(planes, lambda step_x, sign: sign == -1 and step_x > 0, keep_back)

    @pl.when(has_high)
    def _():
        above[0].start()
        below[2].wait_recv()

    force_on(planes + 1, lambda step_x, sign: sign == -1 and step_x == 2, keep_far)

    @pl.when(has_high)
    def _():
        above[1].start()

    ride_both(3)
    load_velocity.wait()
    force_on(1, lambda step_x, sign: sign == 1 or step_x <= 1, keep_partial(1))

    @pl.when(has_low)
    def _():
        above[0].wait_recv()

    for component in range(3):
        total = partial[0, component] + returned[component]
        ready_velocity[component] = velocity[component, 0] + 0.1 * total
    ride_both(4)

    @pl.when(has_low)
    def _():
        above[1].wait_recv()
        for copy in below:
            copy.wait_send()

    @pl.when(has_high)
    def _():
        for copy in above:
            copy.wait_send()

    for component in range(3):
        total = partial[1, component]
        if component == 0:
            total = total + returned[3]
        new = velocity[component, 1] + 0.1 * total
        result[3 + component, 1] = new
        result[component, 1] = fields[PLACE[component], 1, 8 : 8 + rows] + 0.1 * new
    ride_both(5)
    bands = rows // BAND
    work = [(plane, band) for plane in range(2, planes) for band in range(bands)]
    for step in range(6, last + 1):
        for pipe in range(PIPES):
            if pipe % 2 == 0 and work:
                plane, band = work.pop(0)
                if plane == planes - 1 and band == 0:
                    shift_plane(planes, False)
                force_on(plane, lambda step_x, sign: True, finish(plane), band, band + 1)
            ride(pipe, step)
    for plane, band in work:
        force_on(plane, lambda step_x, sign: True, finish(plane), band, band + 1)


def on_device(displacement, velocity, damage, broken, counts, bits):
    planes, rows, cells = damage.shape
    half = cells // 2
    vmem = pl.BlockSpec(memory_space=pltpu.VMEM)
    smem = pl.BlockSpec(memory_space=pltpu.SMEM)
    hbm = pl.BlockSpec(memory_space=pltpu.HBM)
    f32, i32 = jnp.float32, jnp.int32
    tall = rows + 16
    return pl.pallas_call(
        kernel,
        out_shape=jax.ShapeDtypeStruct((6, planes, rows, cells), f32),
        in_specs=[smem] * 2 + [hbm] * 4,
        out_specs=vmem,
        scratch_shapes=[
            pltpu.VMEM((4, planes + 2, tall, cells), f32),
            pltpu.VMEM((2, planes, tall, cells), i32),
            pltpu.VMEM((3, planes, rows, cells), f32),
            pltpu.VMEM((4, planes + 1, tall, cells), f32),
            pltpu.VMEM((4, planes + 1, tall, cells), f32),
            pltpu.VMEM((2, planes, tall, cells), i32),
            pltpu.VMEM((2, planes, tall, cells), i32),
            pltpu.VMEM((3, 4, planes + 1, rows, cells), f32),
            pltpu.VMEM((3, 4, planes + 1, rows, cells), f32),
            pltpu.VMEM((3, 2, planes, rows, cells), i32),
            pltpu.VMEM((3, 2, planes, rows, cells), i32),
            pltpu.VMEM((2, planes, rows, cells), f32),
            pltpu.VMEM((2, planes, rows, cells), f32),
            pltpu.VMEM((planes, rows, cells), i32),
            pltpu.VMEM((2, 3, rows, cells), f32),
            pltpu.VMEM((4, rows, cells), f32),
            pltpu.VMEM((4, rows, cells), f32),
            pltpu.VMEM((PIPES, ROUNDS, 3, 8, half), f32),
            pltpu.VMEM((3, rows, cells), f32),
            pltpu.VMEM((3, rows, cells), f32),
        ]
        + [pltpu.VMEM((ROUNDS, 3, 8, half), f32)] * (4 * PIPES)
        + [
            pltpu.SemaphoreType.DMA((2,)),
            pltpu.SemaphoreType.DMA((2,)),
            pltpu.SemaphoreType.DMA((3,)),
            pltpu.SemaphoreType.DMA((3,)),
            pltpu.SemaphoreType.DMA((2,)),
            pltpu.SemaphoreType.DMA((2,)),
            pltpu.SemaphoreType.DMA((PIPES, 2, ROUNDS)),
            pltpu.SemaphoreType.DMA((PIPES, 2, ROUNDS)),
            pltpu.SemaphoreType.DMA((6,)),
        ],
        compiler_params=pltpu.CompilerParams(
            collective_id=0, has_side_effects=True, vmem_limit_bytes=60 * 1024 * 1024
        ),
    )(counts.T, bits, displacement, velocity, damage, broken)


def solution(mesh):
    return jax.shard_map(
        on_device,
        mesh=mesh,
        in_specs=(
            P(None, "slab", "col", None),
            P(None, "slab", "col", None),
            P("slab", "col", None),
            P(None, "slab", "col", None),
            P(),
            P(),
        ),
        out_specs=P(None, "slab", "col", None),
        check_vma=False,
    )
```

```python
import functools
import math

import jax
import jax.numpy as jnp
from jax import lax
from jax.experimental import pallas as pl
from jax.experimental.pallas import tpu as pltpu
from jax.sharding import PartitionSpec as P

MESH = pl.DeviceIdType.MESH
PLACE = (0, 2, 3)
BAND = 16
ROUNDS = 4
PIPES = 4
PARTS = 4


def bond_table():
    table = []
    for step_x in range(-2, 3):
        for step_y in range(-2, 3):
            for step_z in range(-2, 3):
                square = step_x * step_x + step_y * step_y + step_z * step_z
                if 0 < square <= 4 and (step_x, step_y, step_z) > (0, 0, 0):
                    length = math.sqrt(square)
                    table.append((step_x, step_y, step_z, (1.0 - length / 2.5) / length**3))
    return table


def moved_along_cells(value, step):
    cells = value.shape[-1]
    lane = lax.broadcasted_iota(jnp.int32, value.shape, value.ndim - 1)
    turned = pltpu.roll(value, (-step) % cells, value.ndim - 1)
    inside = (lane < cells - step) if step > 0 else (lane >= -step)
    return jnp.where(inside, turned, jnp.zeros_like(turned))


def kernel(
    counts, bits, displacement, velocity_in, damage, broken, written,
    result, fields, flags, velocity, fields_low, fields_high, flags_low, flags_high,
    rows_low, rows_high, row_flags_low, row_flags_high, far_low, far_high, far_flags,
    partial, back, returned, stage, arrived, ready_velocity, *rest,
):
    buffers, rest = rest[: 4 * PIPES], rest[4 * PIPES :]
    (
        col_send, col_recv, down_send, down_recv, back_send, back_recv,
        ride_send, ride_recv, load_done, write_done,
    ) = rest
    planes, rows, cells = damage.shape
    half = cells // 2
    slabs = lax.axis_size("slab")
    slab = lax.axis_index("slab")
    col = lax.axis_index("col")
    other = 1 - col
    has_low = slab > 0
    has_high = slab < slabs - 1
    table = bond_table()
    incoming = [buffers[2 * pipe : 2 * pipe + 2] for pipe in range(PIPES)]
    outgoing = [buffers[2 * (PIPES + pipe) : 2 * (PIPES + pipe) + 2] for pipe in range(PIPES)]

    inner = pl.ds(8, rows)
    loads = [
        pltpu.make_async_copy(
            displacement.at[component], fields.at[PLACE[component], 0:planes, inner],
            load_done.at[component],
        )
        for component in range(3)
    ]
    loads.append(
        pltpu.make_async_copy(damage, fields.at[1, 0:planes, inner], load_done.at[3])
    )
    load_flags = pltpu.make_async_copy(broken, flags.at[:, :, inner], load_done.at[4])
    load_velocity = pltpu.make_async_copy(velocity_in, velocity, load_done.at[5])
    for copy in loads + [load_flags, load_velocity]:
        copy.start()
    fields[:, 0:planes, 0:8] = jnp.zeros((4, planes, 8, cells), jnp.float32)
    fields[:, 0:planes, 8 + rows : 16 + rows] = jnp.zeros((4, planes, 8, cells), jnp.float32)
    fields[:, planes : planes + 2] = jnp.zeros((4, 2, rows + 16, cells), jnp.float32)
    flags[:, :, 0:8] = jnp.zeros((2, planes, 8, cells), jnp.int32)
    flags[:, :, 8 + rows : 16 + rows] = jnp.zeros((2, planes, 8, cells), jnp.int32)
    returned[...] = jnp.zeros_like(returned)
    stage[...] = jnp.zeros_like(stage)

    partners = []
    for bit in range(ROUNDS):
        weight = 1 << bit
        partners.append(slab + weight - 2 * weight * ((slab // weight) % 2))

    taken, rounds_of = [], []
    for number in range(ROUNDS):
        partner = partners[0]
        for bit in range(1, ROUNDS):
            partner = jnp.where(bits[number] == bit, partners[bit], partner)
        taken.append(jnp.minimum(counts[number, slab], counts[number, partner]))
    for bit in range(ROUNDS):
        place = jnp.int32(0)
        for number in range(1, ROUNDS):
            place = jnp.where(bits[number] == bit, number, place)
        rounds_of.append(place)

    barrier = pltpu.get_barrier_semaphore()

    def greet(to_slab, to_col):
        pl.semaphore_signal(barrier, inc=1, device_id=(to_slab, to_col), device_id_type=MESH)

    greet(slab, other)
    for partner in partners:
        greet(partner, col)

    @pl.when(has_low)
    def _():
        greet(slab - 1, col)
        greet(slab - 1, other)

    @pl.when(has_high)
    def _():
        greet(slab + 1, col)
        greet(slab + 1, other)

    sides = has_low.astype(jnp.int32) + has_high.astype(jnp.int32)
    pl.semaphore_wait(barrier, 1 + ROUNDS + 2 * sides)

    rim = pl.ds(pl.multiple_of(8 + (1 - col) * (rows - 8), 8), 8)
    ghost = pl.ds(pl.multiple_of((8 + rows) * col, 8), 8)

    def remote(source, target, sends, receives, to_slab, to_col):
        return pltpu.make_async_remote_copy(
            src_ref=source, dst_ref=target, send_sem=sends, recv_sem=receives,
            device_id=(to_slab, to_col), device_id_type=MESH,
        )

    beside = [
        remote(fields.at[:, 0:planes, rim], fields.at[:, 0:planes, ghost],
               col_send.at[0], col_recv.at[0], slab, other),
        remote(flags.at[:, :, rim], flags.at[:, :, ghost],
               col_send.at[1], col_recv.at[1], slab, other),
    ]
    below = [
        remote(fields.at[:, 0, inner], fields.at[:, planes, inner],
               down_send.at[0], down_recv.at[0], slab - 1, col),
        remote(fields.at[:, 0, rim], fields.at[:, planes, ghost],
               down_send.at[1], down_recv.at[1], slab - 1, other),
        remote(fields.at[0:2, 1, inner], fields.at[0:2, planes + 1, inner],
               down_send.at[2], down_recv.at[2], slab - 1, col),
    ]
    above = [
        remote(back.at[0:3], returned.at[0:3], back_send.at[0], back_recv.at[0], slab + 1, col),
        remote(back.at[3], returned.at[3], back_send.at[1], back_recv.at[1], slab + 1, col),
    ]

    for copy in loads:
        copy.wait()

    @pl.when(has_low)
    def _():
        for copy in below[0:2]:
            copy.start()

    beside[0].start()
    load_flags.wait()
    beside[1].start()

    column = lax.broadcasted_iota(jnp.int32, (3, 8, half), 1)

    def rides(pipe, step):
        parity = step % 2
        return [
            remote(outgoing[pipe][parity].at[bit], incoming[pipe][parity].at[bit],
                   ride_send.at[pipe, parity, bit], ride_recv.at[pipe, parity, bit],
                   partners[bit], col)
            for bit in range(ROUNDS)
        ]

    last = 2 * PARTS + ROUNDS - 1
    share = rows // PIPES
    writes = [
        pltpu.make_async_copy(
            result.at[:, 0, pl.ds(pipe * share, share)],
            written.at[:, 0, pl.ds(pipe * share, share)], write_done.at[pipe],
        )
        for pipe in range(PIPES)
    ]
    writes += [
        pltpu.make_async_copy(
            result.at[:, plane], written.at[:, plane], write_done.at[PIPES + plane - 1]
        )
        for plane in range(1, planes)
    ]

    def ride(pipe, step):
        def spot(item):
            part = item % PARTS
            first = pipe * (rows // PIPES) + (part // 2) * 8
            return slice(first, first + 8), slice(part % 2 * half, (part % 2 + 1) * half)

        if step > 0:
            for copy in rides(pipe, step - 1):
                copy.wait_recv()
            source = incoming[pipe][(step - 1) % 2]
            for number in reversed(range(ROUNDS)):
                item = step - 1 - number
                if not 0 <= item < 2 * PARTS:
                    continue
                where, lanes = spot(item)
                new = jnp.where(
                    column < taken[number] - where.start,
                    source[bits[number]], stage[pipe, number],
                )
                if number < ROUNDS - 1:
                    stage[pipe, number + 1] = new
                elif item < PARTS:
                    arrived[:, where, lanes] = new
                else:
                    result[3:6, 0, where, lanes] = new
                    result[0:3, 0, where, lanes] = arrived[:, where, lanes] + 0.1 * new
        if step < last:
            if step < 2 * PARTS:
                where, lanes = spot(step)
                if step < PARTS:
                    tall = slice(where.start + 8, where.stop + 8)
                    for component in range(3):
                        stage[pipe, 0, component] = fields[PLACE[component], 0, tall, lanes]
                else:
                    stage[pipe, 0] = ready_velocity[:, where, lanes]
            if step >= 2:
                for copy in rides(pipe, step - 2):
                    copy.wait_send()
            target = outgoing[pipe][step % 2]
            for bit in range(ROUNDS):
                target[bit] = stage[pipe, rounds_of[bit]]
            for copy in rides(pipe, step):
                copy.start()
        else:
            writes[pipe].start()
            for back_step in (last - 2, last - 1):
                for copy in rides(pipe, back_step):
                    copy.wait_send()

    def ride_both(step):
        for pipe in range(PIPES):
            ride(pipe, step)

    def shift_plane(plane, with_flags):
        for field in range(4):
            value = fields[field, plane]
            fields_low[field, plane] = moved_along_cells(value, -1)
            fields_high[field, plane] = moved_along_cells(value, 1)
        if with_flags:
            for part in range(2):
                value = flags[part, plane]
                flags_low[part, plane] = moved_along_cells(value, -1)
                flags_high[part, plane] = moved_along_cells(value, 1)

        def field_rows(field, carry):
            for place, source in enumerate((fields_low, fields, fields_high)):
                rows_low[place, field, plane] = source[field, plane, 7 : 7 + rows]
                rows_high[place, field, plane] = source[field, plane, 9 : 9 + rows]
            return carry

        lax.fori_loop(0, 4, field_rows, 0)
        if with_flags:

            def flag_rows(part, carry):
                for place, source in enumerate((flags_low, flags, flags_high)):
                    row_flags_low[place, part, plane] = source[part, plane, 7 : 7 + rows]
                    row_flags_high[place, part, plane] = source[part, plane, 9 : 9 + rows]
                return carry

            lax.fori_loop(0, 2, flag_rows, 0)
            for field in range(2):
                far_low[field, plane] = fields[field + 1, plane, 6 : 6 + rows]
                far_high[field, plane] = fields[field + 1, plane, 10 : 10 + rows]
            far_flags[plane] = flags[0, plane, 6 : 6 + rows]

    def force_on(plane, choose, emit, first=0, stop=rows // BAND):
        def body(index, carry):
            start = pl.multiple_of(index * BAND, 8)
            own_rows = pl.ds(start + 8, BAND)
            own = [fields[field, plane, own_rows] for field in range(4)]
            force = [jnp.zeros((BAND, cells), jnp.float32) for _ in range(3)]
            for number, (step_x, step_y, step_z, weight) in enumerate(table):
                for sign in (1, -1):
                    if not choose(step_x, sign):
                        continue
                    step = (sign * step_x, sign * step_y, sign * step_z)
                    there = plane + step[0]

                    def load(plain, low, high, less, more, far_less, far_more, first):
                        if step[1] == -2:
                            return far_less(first, there)
                        if step[1] == 2:
                            return far_more(first, there)
                        if step[1] != 0:
                            shifted = less if step[1] < 0 else more
                            return shifted[step[2] + 1, first, there, pl.ds(start, BAND)]
                        if step[2] == 0:
                            return plain[first, there, own_rows]
                        if step[2] == 1:
                            return high[first, there, own_rows]
                        if step[2] == -1:
                            return low[first, there, own_rows]
                        return moved_along_cells(plain[first, there, own_rows], step[2])

                    def field_at(first):
                        return load(
                            fields, fields_low, fields_high, rows_low, rows_high,
                            lambda f, p: far_low[f - 1, p, pl.ds(start, BAND)],
                            lambda f, p: far_high[f - 1, p, pl.ds(start, BAND)],
                            first,
                        )

                    along = None
                    for component in range(3):
                        if step[component] == 0:
                            continue
                        part = field_at(PLACE[component])
                        part = part - own[PLACE[component]]
                        if step[component] < 0:
                            part = -part
                        along = part if along is None else along + part
                    size = 2.0 if max(abs(s) for s in step) == 2 else 1.0
                    scale = field_at(1)
                    if sign == 1:
                        source = flags[number // 8, plane, own_rows]
                    else:
                        source = load(
                            flags, flags_low, flags_high, row_flags_low, row_flags_high,
                            lambda f, p: far_flags[p, pl.ds(start, BAND)], None, number // 8,
                        )
                    factor = (weight * size * size) * scale * along
                    factor = jnp.where(
                        jnp.bitwise_and(source, 1 << (number % 8)) == 0, factor, 0.0
                    )
                    for component in range(3):
                        if step[component] > 0:
                            force[component] = force[component] + factor
                        elif step[component] < 0:
                            force[component] = force[component] - factor
            emit(pl.ds(start, BAND), [own[1] * total for total in force])
            return carry

        lax.fori_loop(first, stop, body, 0)

    def keep_partial(plane):
        def emit(where, force):
            for component in range(3):
                partial[plane, component, where] = force[component]
        return emit

    def finish(plane):
        def emit(where, force):
            for component in range(3):
                new = velocity[component, plane, where] + 0.1 * force[component]
                result[3 + component, plane, where] = new
                result[component, plane, where] = (
                    fields[PLACE[component], plane, pl.ds(where.start + 8, BAND)] + 0.1 * new
                )
        return emit

    def keep_back(where, force):
        for component in range(3):
            back[component, where] = force[component]

    def keep_far(where, force):
        back[3, where] = force[0]

    ride_both(0)
    for copy in beside:
        copy.wait()

    @pl.when(has_low)
    def _():
        below[2].start()

    ride_both(1)

    def shift_own(plane, carry):
        shift_plane(plane, True)
        return carry

    lax.fori_loop(0, planes, shift_own, 0)
    ride_both(2)
    force_on(0, lambda step_x, sign: sign == 1 or step_x == 0, keep_partial(0))

    @pl.when(has_high)
    def _():
        for copy in below[0:2]:
            copy.wait_recv()

    force_on(planes, lambda step_x, sign: sign == -1 and step_x > 0, keep_back)

    @pl.when(has_high)
    def _():
        above[0].start()
        below[2].wait_recv()

    force_on(planes + 1, lambda step_x, sign: sign == -1 and step_x == 2, keep_far)

    @pl.when(has_high)
    def _():
        above[1].start()

    ride_both(3)
    load_velocity.wait()
    force_on(1, lambda step_x, sign: sign == 1 or step_x <= 1, keep_partial(1))

    @pl.when(has_low)
    def _():
        above[0].wait_recv()

    for component in range(3):
        total = partial[0, component] + returned[component]
        ready_velocity[component] = velocity[component, 0] + 0.1 * total
    ride_both(4)

    @pl.when(has_low)
    def _():
        above[1].wait_recv()
        for copy in below:
            copy.wait_send()

    @pl.when(has_high)
    def _():
        for copy in above:
            copy.wait_send()

    for component in range(3):
        total = partial[1, component]
        if component == 0:
            total = total + returned[3]
        new = velocity[component, 1] + 0.1 * total
        result[3 + component, 1] = new
        result[component, 1] = fields[PLACE[component], 1, 8 : 8 + rows] + 0.1 * new
    writes[PIPES].start()
    ride_both(5)
    bands = rows // BAND
    step = 6
    for plane in range(2, planes):
        if plane == planes - 1:
            shift_plane(planes, False)
        for part in range(2):
            force_on(
                plane, lambda step_x, sign: True, finish(plane),
                part * bands // 2, (part + 1) * bands // 2,
            )
            if part == 1:
                writes[PIPES + plane - 1].start()
            ride_both(step)
            step += 1
    for step in range(step, last + 1):
        ride_both(step)
    for copy in writes:
        copy.wait()


def on_device(displacement, velocity, damage, broken, counts, bits):
    planes, rows, cells = damage.shape
    half = cells // 2
    smem = pl.BlockSpec(memory_space=pltpu.SMEM)
    hbm = pl.BlockSpec(memory_space=pltpu.HBM)
    f32, i32 = jnp.float32, jnp.int32
    tall = rows + 16
    return pl.pallas_call(
        kernel,
        out_shape=jax.ShapeDtypeStruct((6, planes, rows, cells), f32),
        in_specs=[smem] * 2 + [hbm] * 4,
        out_specs=hbm,
        scratch_shapes=[
            pltpu.VMEM((6, planes, rows, cells), f32),
            pltpu.VMEM((4, planes + 2, tall, cells), f32),
            pltpu.VMEM((2, planes, tall, cells), i32),
            pltpu.VMEM((3, planes, rows, cells), f32),
            pltpu.VMEM((4, planes + 1, tall, cells), f32),
            pltpu.VMEM((4, planes + 1, tall, cells), f32),
            pltpu.VMEM((2, planes, tall, cells), i32),
            pltpu.VMEM((2, planes, tall, cells), i32),
            pltpu.VMEM((3, 4, planes + 1, rows, cells), f32),
            pltpu.VMEM((3, 4, planes + 1, rows, cells), f32),
            pltpu.VMEM((3, 2, planes, rows, cells), i32),
            pltpu.VMEM((3, 2, planes, rows, cells), i32),
            pltpu.VMEM((2, planes, rows, cells), f32),
            pltpu.VMEM((2, planes, rows, cells), f32),
            pltpu.VMEM((planes, rows, cells), i32),
            pltpu.VMEM((2, 3, rows, cells), f32),
            pltpu.VMEM((4, rows, cells), f32),
            pltpu.VMEM((4, rows, cells), f32),
            pltpu.VMEM((PIPES, ROUNDS, 3, 8, half), f32),
            pltpu.VMEM((3, rows, cells), f32),
            pltpu.VMEM((3, rows, cells), f32),
        ]
        + [pltpu.VMEM((ROUNDS, 3, 8, half), f32)] * (4 * PIPES)
        + [
            pltpu.SemaphoreType.DMA((2,)),
            pltpu.SemaphoreType.DMA((2,)),
            pltpu.SemaphoreType.DMA((3,)),
            pltpu.SemaphoreType.DMA((3,)),
            pltpu.SemaphoreType.DMA((2,)),
            pltpu.SemaphoreType.DMA((2,)),
            pltpu.SemaphoreType.DMA((PIPES, 2, ROUNDS)),
            pltpu.SemaphoreType.DMA((PIPES, 2, ROUNDS)),
            pltpu.SemaphoreType.DMA((6,)),
            pltpu.SemaphoreType.DMA((PIPES + planes - 1,)),
        ],
        compiler_params=pltpu.CompilerParams(
            collective_id=0, has_side_effects=True, vmem_limit_bytes=60 * 1024 * 1024
        ),
    )(counts.T, bits, displacement, velocity, damage, broken)


def solution(mesh):
    return jax.shard_map(
        on_device,
        mesh=mesh,
        in_specs=(
            P(None, "slab", "col", None),
            P(None, "slab", "col", None),
            P("slab", "col", None),
            P(None, "slab", "col", None),
            P(),
            P(),
        ),
        out_specs=P(None, "slab", "col", None),
        check_vma=False,
    )
```
